256 devices in a mesh: rep: 16 (over x, z_lo), tp: 16 (over y, z_hi, core).
Axes of the slice: x: 4, y: 4, z: 8 (z_hi: 2, z_lo: 4; z = z_hi * 4 + z_lo), core: 2. Of those that a mesh axis runs over, the one named last changes fastest.
Arguments:
- features: bfloat16 [32768, 2560], P(('rep', 'tp')), may hold values from -24 to 24
- cotangent: bfloat16 [32768, 14336], P('rep', 'tp'), may hold values from -0.59765625 to 0.59765625
- master: float32 [2560, 14336], P(('rep', 'tp')), may hold values from -6 to 6
- first_moment: float32 [2560, 14336], P(('rep', 'tp')), may hold values from -3 to 3
- second_moment: float32 [2560, 14336], P(('rep', 'tp')), may hold values from 0.1 to 4
Outputs:
- new_master: float32 [2560, 14336], P(('rep', 'tp'))
- new_first: float32 [2560, 14336], P(('rep', 'tp'))
- new_second: float32 [2560, 14336], P(('rep', 'tp'))
- new_weights: bfloat16 [2560, 14336], P(None, 'tp')
The draws below stay inside these ranges and needn't reach their ends.
All inputs are finite; a program needn't handle non-finite values.
Results may differ from the reference program's by a relative error of at most 0.0059.
Values may be sent and summed in bfloat16 or wider, within the bound.
No kernel may reach another device: no remote copies, remote signals or barrier semaphores. Data moves between devices by JAX's collectives and lax.ppermute only.
A program may use at most 64 MiB of HBM per device.

```python
import math
import jax
import jax.numpy as jnp
from jax import lax

D = 2560
FF = 14336
TOK = 2048
STEP = 10
TOKENS = 32768
N_REP = 16


def with_spikes(entries, key, source, target, blocks, factor):
    owner, partner = [(jnp.arange(entries.shape[axis_at]) // (entries.shape[axis_at] // blocks)).reshape([-1 if axis == axis_at else 1 for axis in range(entries.ndim)]) for axis_at in (source, target)]
    chosen = jax.random.permutation(key, blocks)[partner]
    strong = (owner == chosen) | (owner == (partner + blocks // 2) % blocks)
    return jnp.where(strong, factor * entries, entries)


def levels(key, extent, cuts, least, high):
    factor_of = 1.0
    for axis_at, parts in cuts:
        heights = jax.random.uniform(jax.random.fold_in(jax.random.fold_in(key, 6), axis_at), (parts,), jnp.float32, least / len(cuts), high / len(cuts))
        factor_of = factor_of * jnp.repeat(jnp.exp(heights), extent[axis_at] // parts).reshape((-1,) + (1,) * (len(extent) - 1 - axis_at))
    return factor_of


def centred(rng, shape, deviation, limit, cuts=(), kind=jnp.bfloat16):
    level = levels(rng, shape, cuts, -0.22, 0.18) if cuts else 1.0
    result = jax.random.normal(rng, shape, jnp.float32) * deviation * level
    return jnp.minimum(jnp.maximum(result, -limit), limit).astype(kind)


def heavy_noise(stream_key, extent, deviation, most, split, heavy, kind=jnp.bfloat16):
    entries = deviation * jax.random.normal(stream_key, extent, jnp.float32)
    if split:
        entries = entries * levels(stream_key, extent, split, -0.22, 0.18)
    return jnp.clip(with_spikes(entries, jax.random.fold_in(stream_key, 3), *heavy), -most, most).astype(kind)


def setup_inputs(seed: int = 0) -> dict:
    arg_keys = jax.random.split(jax.random.key(seed), 6)
    features = heavy_noise(arg_keys[0], (TOKENS, D), 1.0, 24.0, ((0, 256),), (0, 1, 256, 6.0))
    cotangent = centred(arg_keys[1], (TOKENS, FF), 0.09, 0.59765625, ((0, 16), (1, 16)))
    master = centred(arg_keys[2], (D, FF), 1.0, 6.0, ((0, 256),), jnp.float32)
    first_moment = centred(arg_keys[3], (D, FF), 0.5, 3.0, ((0, 256),), jnp.float32)
    second_moment = jnp.clip(jnp.exp(math.log(4.0) - 3.6888794 * jax.random.uniform(arg_keys[4], (D, FF), jnp.float32) ** levels(arg_keys[4], (D, FF), ((0, 256),), -0.2, 0.2)), 0.1, 4.0)
    return {"features": features, "cotangent": cotangent, "master": master, "first_moment": first_moment, "second_moment": second_moment}


beta_one = 0.9
beta_two = 0.95
outer_rate = 0.05
weight_decay = 0.1
epsilon = 1e-08

def reference(features, cotangent, master, first_moment, second_moment):
    inputs = features.reshape(N_REP, TOK, D)
    grads = cotangent.reshape(N_REP, TOK, FF)

    def add_replica(total, pair):
        left = pair[0].astype(jnp.float32)
        right = pair[1].astype(jnp.float32)
        term = jnp.dot(left.T, right, preferred_element_type=jnp.float32).astype(jnp.bfloat16)
        term = lax.optimization_barrier(term)
        return (total + term.astype(jnp.float32), None)
    total, unused = lax.scan(add_replica, jnp.zeros((D, FF), jnp.float32), (inputs, grads))
    pseudo = total / N_REP
    new_first = beta_one * first_moment + (1.0 - beta_one) * pseudo
    new_second = beta_two * second_moment + (1.0 - beta_two) * pseudo * pseudo
    lead = (beta_one * new_first + (1.0 - beta_one) * pseudo) / (1.0 - beta_one ** (STEP + 1))
    scale = new_second / (1.0 - beta_two ** STEP)
    new_master = master - outer_rate * (lead / (jnp.sqrt(scale) + epsilon) + weight_decay * master)
    return (new_master, new_first, new_second, new_master.astype(jnp.bfloat16))
```

```python
import functools

import jax
import jax.numpy as jnp
import numpy as np
from jax import lax
from jax.experimental import pallas as pl
from jax.experimental.pallas import tpu as pltpu
from jax.sharding import PartitionSpec as P

STEP = 10

beta_one = 0.9
beta_two = 0.95
outer_rate = 0.05
weight_decay = 0.1
epsilon = 1e-08

BOTH = ("rep", "tp")
BF16, F32 = jnp.bfloat16, jnp.float32
MIB = 1024 * 1024
SMEM = pl.BlockSpec(memory_space=pltpu.SMEM)
VMEM = pl.BlockSpec(memory_space=pltpu.VMEM)
ANY = pl.BlockSpec(memory_space=pl.ANY)
HBM = pl.BlockSpec(memory_space=pltpu.HBM)

ACROSS = (2, 1, 3, 0)
CHUNKS = (((0, 1), (1, 1)), ((3, 1), (2, 1)), ((2, 0), (1, 0)), ((3, 0), (0, 0)))
ALONE = ((0,), (1,), (2,), (3,))
CUTS = {2: ((0, 2), (1, 3)), 1: ALONE, 3: ALONE, 0: ALONE}
MATES = tuple((dy, dc) for dy in range(4) for dc in range(2))
GROUPS = [[y * 4 + zhi * 2 + core for y in range(4) for core in range(2)] for zhi in range(2)]
PAIRS = ((0, 1), (2, 3))


def facts():
    rows = []
    for rep in range(16):
        for tp in range(16):
            x, zlo = rep // 4, rep % 4
            row = [x, zlo, tp // 4, tp // 2 % 2, tp % 2]
            row += [
                ((x + dx) % 4 * 4 + (zlo - j) % 4) * 160 for pair in PAIRS for dx in (0, 3, 1, 2) for j in pair
            ]
            rows.append(row)
    return np.asarray(rows, np.int32)


X, ZLO, Y, ZHI, CORE, PLACE = 0, 1, 2, 3, 4, 5


def pairs(move):
    def index(x, z, y, c):
        x, z, y, c = x % 4, z % 8, y % 4, c % 2
        return (x * 4 + z % 4) * 16 + y * 4 + (z // 4) * 2 + c

    return [
        (index(x, z, y, c), index(*move(x, z, y, c)))
        for x in range(4)
        for z in range(8)
        for y in range(4)
        for c in range(2)
    ]


def send(value, dx=0, dz=0, dy=0, dc=0):
    return lax.ppermute(value, BOTH, pairs(lambda x, z, y, c: (x + dx, z + dz, y + dy, c + dc)))


def send_z(value, j, h):
    def move(x, z, y, c):
        return x, (z // 4 ^ h) * 4 + (z + j) % 4, y, c

    return lax.ppermute(value, BOTH, pairs(move))


def call(kernel, name, out_shape, in_specs, out_specs, args, scratch=(), limit=16):
    return pl.pallas_call(
        kernel,
        out_shape=out_shape,
        in_specs=in_specs,
        out_specs=out_specs,
        scratch_shapes=list(scratch),
        compiler_params=pltpu.CompilerParams(vmem_limit_bytes=limit * MIB),
        cost_estimate=pl.CostEstimate(flops=0, bytes_accessed=1024, transcendentals=0),
        name=name,
    )(*args)


def prepare_kernel(info, rows, out, half_a, half_b, turned, ordered):
    for k in range(20):
        turned[k * 128 : (k + 1) * 128, :] = rows[:, k * 128 : (k + 1) * 128].astype(F32).T
    at = 0
    for dx in ACROSS:
        for j in range(4):
            start = lax.rem(info[X] + dx, 4) * 640 + lax.rem(info[ZLO] + j, 4) * 160
            for zhi in range(2):
                for y in range(4):
                    ordered[at : at + 20, :] = turned[pl.ds(start + y * 40 + zhi * 20, 20), :]
                    at += 20
    half_a[...] = ordered[:1280, :].astype(BF16)
    half_b[...] = ordered[1280:, :].astype(BF16)
    out[...] = ordered[...].astype(BF16)


def prepare(info, features):
    return call(
        prepare_kernel,
        "prepare",
        [jax.ShapeDtypeStruct((2560, 128), BF16)] + [jax.ShapeDtypeStruct((1280, 128), BF16)] * 2,
        [SMEM, VMEM],
        [VMEM] * 3,
        (info, features),
        [pltpu.VMEM((2560, 128), F32), pltpu.VMEM((2560, 128), F32)],
    )


def term_kernel(dx, info, own, far, g, *refs):
    cuts = CUTS[dx]
    outs = refs[: len(cuts)]
    rows, total, sem = refs[len(cuts) :]
    n = ACROSS.index(dx)
    for source, first, half in ((own, n * 640, info[ZHI]), (far, n % 2 * 640, 1 - info[ZHI])):
        for y in range(4):
            for core in range(2):
                column = pl.multiple_of(y * 512 + half * 256 + core * 128, 128)
                pltpu.make_async_copy(
                    source.at[y * 2 + core, pl.ds(first, 640), :], rows.at[:, pl.ds(column, 128)], sem
                ).start()
    pltpu.make_async_copy(rows, rows, sem).wait()
    for start in range(0, 896, 256):
        stop = min(start + 256, 896)
        total[:, start:stop] = jnp.dot(rows[...], g[:, start:stop], preferred_element_type=F32)
    for out, cut in zip(outs, cuts):
        pieces = [piece for chunk in cut for piece in CHUNKS[chunk]]
        for k, (j, h) in enumerate(pieces):
            at = pl.multiple_of(j * 160 + lax.rem(info[ZHI] + h, 2) * 80, 16)
            out[k * 80 : (k + 1) * 80, :] = total[pl.ds(at, 80), :].astype(BF16)


def term_rows(dx, info, own, far, g):
    return call(
        functools.partial(term_kernel, dx),
        "term_rows",
        [jax.ShapeDtypeStruct((160 * len(cut), 896), BF16) for cut in CUTS[dx]],
        [SMEM, HBM, HBM, VMEM],
        [VMEM] * len(CUTS[dx]),
        (info, own, far, g),
        [pltpu.VMEM((640, 2048), BF16), pltpu.VMEM((640, 896), F32), pltpu.SemaphoreType.DMA],
        limit=56,
    )


def collect_kernel(info, *refs):
    parts, outs, total = refs[:8], refs[8:16], refs[16]
    for h in range(2):
        block = [parts[4 * h + j][...].astype(F32) for j in range(4)]
        block = (block[0] + block[1]) + (block[2] + block[3])
        for k in range(8):
            total[h, k] = block[k * 10 : (k + 1) * 10, :]
    for (dy, dc), out in zip(MATES, outs):
        at = lax.rem(info[Y] + dy, 4) * 2 + lax.rem(info[CORE] + dc, 2)
        for h in range(2):
            out[h] = total[h, at].astype(BF16)


def collect(info, parts):
    return call(
        collect_kernel,
        "collect",
        [jax.ShapeDtypeStruct((2, 10, 896), BF16)] * 8,
        [SMEM] + [VMEM] * 8,
        [VMEM] * 8,
        (info, *parts),
        [pltpu.VMEM((2, 8, 10, 896), F32)],
    )


def update_kernel(info, *refs):
    parts, (master, first, second) = refs[:8], refs[8:11]
    new_master, new_first, new_second = refs[11:14]
    fresh = refs[14:]
    for (dy, dc), part, out in zip(MATES, parts, fresh):
        for h in range(2):
            column = (
                lax.rem(info[Y] + 4 - dy, 4) * 4
                + lax.rem(info[ZHI] + h, 2) * 2
                + lax.rem(info[CORE] + dc, 2)
            ) * 896
            block = (slice(None), pl.ds(pl.multiple_of(column, 128), 896))
            pseudo = part[h].astype(F32) / 16.0
            old = master[block]
            moved = beta_one * first[block] + (1.0 - beta_one) * pseudo
            spread = beta_two * second[block] + (1.0 - beta_two) * pseudo * pseudo
            lead = (beta_one * moved + (1.0 - beta_one) * pseudo) / (1.0 - beta_one ** (STEP + 1))
            scale = spread / (1.0 - beta_two**STEP)
            value = old - outer_rate * (lead / (jnp.sqrt(scale) + epsilon) + weight_decay * old)
            new_master[block] = value
            new_first[block] = moved
            new_second[block] = spread
            out[h] = value.astype(BF16)


def update(info, parts, master, first, second):
    return call(
        update_kernel,
        "update",
        [jax.ShapeDtypeStruct((10, 14336), F32)] * 3 + [jax.ShapeDtypeStruct((2, 10, 896), BF16)] * 8,
        [SMEM] + [VMEM] * 11,
        [VMEM] * 11,
        (info, *parts, master, first, second),
    )


def weave_kernel(info, *refs):
    parts, outs, groups, rows = refs[:8], refs[8:10], refs[10], refs[11]
    for (dy, dc), part in zip(MATES, parts):
        at = lax.rem(info[Y] + 4 - dy, 4) * 2 + lax.rem(info[CORE] + dc, 2)
        for h in range(2):
            groups[h, at] = part[h].astype(F32)
    for h, out in enumerate(outs):
        for k in range(8):
            rows[h, k * 10 : (k + 1) * 10, :] = groups[h, k]
        out[...] = rows[h].astype(BF16)


def weave(info, parts):
    return call(
        weave_kernel,
        "weave",
        [jax.ShapeDtypeStruct((80, 896), BF16)] * 2,
        [SMEM] + [VMEM] * 8,
        [VMEM] * 2,
        (info, *parts),
        [pltpu.VMEM((2, 8, 10, 896), F32), pltpu.VMEM((2, 80, 896), F32)],
    )


def merge_kernel(info, *refs):
    parts, out, rows = refs[:4], refs[4], refs[5]
    low = info[ZHI] == 0
    for n in range(2):
        mine, far = parts[2 * n][...].astype(F32), parts[2 * n + 1][...].astype(F32)
        for k, block in enumerate((jnp.where(low, mine, far), jnp.where(low, far, mine))):
            for y in range(4):
                at = n * 160 + y * 40 + k * 20
                rows[at : at + 20, :] = block[y * 20 : (y + 1) * 20, :]
    out[...] = rows[...].astype(BF16)


def merge(info, parts):
    return call(
        merge_kernel,
        "merge",
        jax.ShapeDtypeStruct((320, 896), BF16),
        [SMEM] + [VMEM] * 4,
        VMEM,
        (info, *parts),
        [pltpu.VMEM((320, 896), F32)],
    )


def place_kernel(info, *refs):
    blocks, out, sem = refs[:10], refs[10], refs[11]
    k = 0
    for block in blocks:
        for first in range(0, block.shape[0], 160):
            at = pl.multiple_of(info[PLACE + k], 32)
            pltpu.make_async_copy(
                block.at[pl.ds(first, 160), :], out.at[pl.ds(at, 160), :], sem
            ).start()
            k += 1
    pltpu.make_async_copy(out, out, sem).wait()


def place(info, blocks):
    return call(
        place_kernel,
        "place",
        jax.ShapeDtypeStruct((2560, 896), BF16),
        [SMEM] + [VMEM] * 10,
        ANY,
        (info, *blocks),
        [pltpu.SemaphoreType.DMA],
    )


def tie(*values):
    return lax.optimization_barrier(values)


def gather(value):
    return lax.all_gather(value, "tp", axis_index_groups=GROUPS, axis=0)


def on_device(features, cotangent, master, first_moment, second_moment):
    device = lax.axis_index("rep") * 16 + lax.axis_index("tp")
    info = lax.dynamic_index_in_dim(jnp.asarray(facts()), device, 0, keepdims=False)

    own, half_a, half_b = prepare(info, features)
    own = gather(own)
    far_a, far_b = tie(send(half_a, dz=2), send(half_b, dz=-2))
    far_a, far_b, own = tie(send(far_a, dz=2), send(far_b, dz=-2), own)
    far_a = gather(far_a)
    far_b, _ = tie(far_b, far_a)
    far_b = gather(far_b)

    def add(first, *others):
        total = first.astype(F32)
        for other in others:
            total = total + other.astype(F32)
        return total.astype(BF16)

    def cut(total, chunk):
        result = {}
        for i, (j, h) in enumerate(CHUNKS[chunk]):
            part = total[i * 80 : (i + 1) * 80]
            result[j, h] = part if (j, h) == (0, 0) else send_z(part, j, h)
        return result

    two_ac, two_bd = term_rows(2, info, own, far_a, cotangent)
    two_ac, two_bd = send(two_ac, dx=1), send(two_bd, dx=-1)
    right = term_rows(1, info, own, far_a, cotangent)
    plain_b = send(right[1], dx=1)
    carried_a = add(right[0], two_ac[:160])
    carried_a, far_b = tie(carried_a, far_b)
    left = term_rows(3, info, own, far_b, cotangent)
    plain_a = send(left[0], dx=-1)
    carried_b = add(left[1], two_bd[:160])
    carried_a, carried_b = send(carried_a, dx=1), send(carried_b, dx=-1)
    plain_d, plain_c, _, _ = tie(right[3], left[2], two_ac, two_bd)
    plain_d, plain_c = send(plain_d, dx=1), send(plain_c, dx=-1)
    here = term_rows(0, info, own, far_b, cotangent)
    carried_c, carried_d = add(right[2], two_ac[160:]), add(left[3], two_bd[160:])
    sum_a, sum_b = add(here[0], plain_a, carried_a), add(here[1], plain_b, carried_b)
    carried_c, carried_d, sum_a, sum_b = tie(carried_c, carried_d, sum_a, sum_b)
    carried_c, carried_d = send(carried_c, dx=1), send(carried_d, dx=-1)
    parts = {**cut(sum_a, 0), **cut(sum_b, 1)}
    parts.update(cut(add(here[2], plain_c, carried_c), 2))
    parts.update(cut(add(here[3], plain_d, carried_d), 3))

    mine = collect(info, [parts[j, h] for h in range(2) for j in range(4)])
    mine = [part if (dy, dc) == (0, 0) else send(part, dy=dy, dc=dc) for (dy, dc), part in zip(MATES, mine)]
    new_master, new_first, new_second, *fresh = update(
        info, mine, master, first_moment, second_moment
    )
    fresh = dict(zip(MATES, fresh))
    fresh = [
        fresh[dy, dc] if (dy, dc) == (0, 0) else send(fresh[-dy % 4, dc], dy=dy, dc=dc) for dy, dc in MATES
    ]
    woven = weave(info, fresh)

    same, other = woven
    block = merge(info, [same, send_z(other, 0, 1), send_z(same, 1, 0), send_z(other, 1, 1)])
    block, same, other = tie(block, same, other)
    left, right = send(block, dx=1), send(block, dx=-1)
    parts = [send_z(value, j, h) for j in (2, 3) for h, value in enumerate((same, other))]
    *parts, left, right = tie(*parts, left, right)
    low, high = send(left[:160], dx=1), send(right[160:], dx=-1)
    blocks = [block, left, right, low, high]
    block = merge(info, parts)
    left, right = send(block, dx=1), send(block, dx=-1)
    low, high = send(left[:160], dx=1), send(right[160:], dx=-1)
    blocks += [block, left, right, low, high]
    new_weights = place(info, blocks)
    return (new_master, new_first, new_second, new_weights)


def solution(mesh):
    in_specs = (
        P(("rep", "tp"), None),
        P("rep", "tp"),
        P(("rep", "tp"), None),
        P(("rep", "tp"), None),
        P(("rep", "tp"), None),
    )
    out_specs = (
        P(("rep", "tp"), None),
        P(("rep", "tp"), None),
        P(("rep", "tp"), None),
        P(None, "tp"),
    )
    return jax.shard_map(
        on_device, mesh=mesh, in_specs=in_specs, out_specs=out_specs, check_vma=False
    )
```

```python
import functools

import jax
import jax.numpy as jnp
import numpy as np
from jax import lax
from jax.experimental import pallas as pl
from jax.experimental.pallas import tpu as pltpu
from jax.sharding import PartitionSpec as P

STEP = 10

beta_one = 0.9
beta_two = 0.95
outer_rate = 0.05
weight_decay = 0.1
epsilon = 1e-08

BOTH = ("rep", "tp")
BF16, F32 = jnp.bfloat16, jnp.float32
MIB = 1024 * 1024
SMEM = pl.BlockSpec(memory_space=pltpu.SMEM)
VMEM = pl.BlockSpec(memory_space=pltpu.VMEM)
ANY = pl.BlockSpec(memory_space=pl.ANY)

ACROSS = (2, 1, 3, 0)
CHUNKS = (((0, 1), (0, 0)), ((2, 0), (2, 1)), ((1, 0), (1, 1)), ((3, 0), (3, 1)))
ALONE = ((0,), (1,), (2,), (3,))
CUTS = {2: ((0, 2), (1, 3)), 1: ALONE, 3: ALONE, 0: ALONE}
PIECES = tuple((dy, dh, dc) for dh in range(2) for dy in (0, 3, 1, 2) for dc in range(2))
PAIRS = ((1, 3), (0, 2))


def facts():
    rows = []
    for rep in range(16):
        for tp in range(16):
            x, zlo = rep // 4, rep % 4
            row = [x, zlo, tp // 4, tp // 2 % 2, tp % 2]
            row += [
                ((x + dx) % 4 * 4 + (zlo - j) % 4) * 160 for pair in PAIRS for dx in (0, 3, 1, 2) for j in pair
            ]
            y, zhi, core = row[2:5]
            row += [((y + dy) % 4 * 4 + (zhi ^ dh) * 2 + (core ^ dc)) * 128 for dy, dh, dc in PIECES]
            rows.append(row)
    return np.asarray(rows, np.int32)


X, ZLO, Y, ZHI, CORE, PLACE, TOKEN = 0, 1, 2, 3, 4, 5, 21


def pairs(move):
    def index(x, z, y, c):
        x, z, y, c = x % 4, z % 8, y % 4, c % 2
        return (x * 4 + z % 4) * 16 + y * 4 + (z // 4) * 2 + c

    return [
        (index(x, z, y, c), index(*move(x, z, y, c)))
        for x in range(4)
        for z in range(8)
        for y in range(4)
        for c in range(2)
    ]


def send(value, dx=0, dz=0, dy=0, dc=0):
    return lax.ppermute(value, BOTH, pairs(lambda x, z, y, c: (x + dx, z + dz, y + dy, c + dc)))


def send_z(value, j, h):
    def move(x, z, y, c):
        return x, (z // 4 ^ h) * 4 + (z + j) % 4, y, c

    return lax.ppermute(value, BOTH, pairs(move))


def call(kernel, name, out_shape, in_specs, out_specs, args, scratch=(), limit=16, size=1024):
    return pl.pallas_call(
        kernel,
        out_shape=out_shape,
        in_specs=in_specs,
        out_specs=out_specs,
        scratch_shapes=list(scratch),
        compiler_params=pltpu.CompilerParams(vmem_limit_bytes=limit * MIB),
        cost_estimate=pl.CostEstimate(flops=0, bytes_accessed=size, transcendentals=0),
        name=name,
    )(*args)


def prepare_kernel(info, rows, out, half_a, half_b, turned, ordered):
    for k in range(20):
        turned[k * 128 : (k + 1) * 128, :] = rows[:, k * 128 : (k + 1) * 128].astype(F32).T
    at = 0
    for dx in ACROSS:
        for j in range(4):
            start = lax.rem(info[X] + dx, 4) * 640 + lax.rem(info[ZLO] + j, 4) * 160
            for zhi in range(2):
                for y in range(4):
                    ordered[at : at + 20, :] = turned[pl.ds(start + y * 40 + zhi * 20, 20), :]
                    at += 20
    half_a[...] = ordered[:1280, :].astype(BF16)
    half_b[...] = ordered[1280:, :].astype(BF16)
    out[...] = ordered[...].astype(BF16)


def prepare(info, features):
    return call(
        prepare_kernel,
        "prepare",
        [jax.ShapeDtypeStruct((2560, 128), BF16)] + [jax.ShapeDtypeStruct((1280, 128), BF16)] * 2,
        [SMEM, VMEM],
        [VMEM] * 3,
        (info, features),
        [pltpu.VMEM((2560, 128), F32), pltpu.VMEM((2560, 128), F32)],
    )


def fetch_kernel(info, g, _, out, sem):
    for k in range(16):
        start = pl.multiple_of(info[TOKEN + k], 128)
        pltpu.make_async_copy(g.at[pl.ds(start, 128), :], out.at[pl.ds(k * 128, 128), :], sem).start()
    pltpu.make_async_copy(out, out, sem).wait()


def fetch(info, g, after):
    return call(
        fetch_kernel,
        "fetch",
        jax.ShapeDtypeStruct((2048, 896), BF16),
        [SMEM, ANY, ANY],
        VMEM,
        (info, g, after),
        [pltpu.SemaphoreType.DMA],
        size=16 * MIB,
    )


def term_kernel(firsts, cuts, info, *refs):
    pieces, g, outs, total = refs[:16], refs[16], refs[17:-1], refs[-1]
    rows = jnp.concatenate([piece[first : first + 640, :] for piece, first in zip(pieces, firsts)], axis=1)
    for start in range(0, 896, 256):
        stop = min(start + 256, 896)
        total[:, start:stop] = jnp.dot(rows, g[:, start:stop], preferred_element_type=F32)
    for out, cut in zip(outs, cuts):
        for k, (j, h) in enumerate(piece for chunk in cut for piece in CHUNKS[chunk]):
            at = pl.multiple_of(j * 160 + lax.rem(info[ZHI] + h, 2) * 80, 16)
            out[k * 80 : (k + 1) * 80, :] = total[pl.ds(at, 80), :].astype(BF16)


def term_rows(dx, info, pieces, g):
    arrays, firsts = zip(*pieces)
    return call(
        functools.partial(term_kernel, firsts, CUTS[dx]),
        "term_rows",
        [jax.ShapeDtypeStruct((160 * len(cut), 896), BF16) for cut in CUTS[dx]],
        [SMEM] + [VMEM] * 17,
        [VMEM] * len(CUTS[dx]),
        (info, *arrays, g),
        [pltpu.VMEM((640, 896), F32)],
        limit=24,
    )


def collect_kernel(info, *refs):
    parts, mine, theirs, total = refs[:8], refs[8], refs[9], refs[10]
    for h in range(2):
        block = [parts[4 * h + j][...].astype(F32) for j in range(4)]
        block = (block[0] + block[1]) + (block[2] + block[3])
        for k in range(8):
            total[h, k] = block[k * 10 : (k + 1) * 10, :]
    for y in range(4):
        for h in range(2):
            mine[y, h] = total[h, 2 * y + info[CORE]].astype(BF16)
            theirs[y, h] = total[h, 2 * y + 1 - info[CORE]].astype(BF16)


def collect(info, parts):
    return call(
        collect_kernel,
        "collect",
        [jax.ShapeDtypeStruct((4, 2, 10, 896), BF16)] * 2,
        [SMEM] + [VMEM] * 8,
        [VMEM] * 2,
        (info, *parts),
        [pltpu.VMEM((2, 8, 10, 896), F32)],
    )


def pack_kernel(info, mine, other, *outs):
    for dy, out in enumerate(outs):
        y = lax.rem(info[Y] + dy, 4)
        out[0] = mine[y]
        out[1] = other[y]


def pack(info, mine, other):
    return call(
        pack_kernel,
        "pack",
        [jax.ShapeDtypeStruct((2, 2, 10, 896), BF16)] * 4,
        [SMEM] + [VMEM] * 2,
        [VMEM] * 4,
        (info, mine, other),
    )


def update_kernel(info, *refs):
    parts, (master, first, second) = refs[:4], refs[4:7]
    new_master, new_first, new_second = refs[7:10]
    fresh = refs[10:]
    for dy, (part, out) in enumerate(zip(parts, fresh)):
        for dc in range(2):
            for h in range(2):
                column = (
                    lax.rem(info[Y] + 4 - dy, 4) * 4
                    + lax.rem(info[ZHI] + h, 2) * 2
                    + lax.rem(info[CORE] + dc, 2)
                ) * 896
                block = (slice(None), pl.ds(pl.multiple_of(column, 128), 896))
                pseudo = part[dc, h].astype(F32) / 16.0
                old = master[block]
                moved = beta_one * first[block] + (1.0 - beta_one) * pseudo
                spread = beta_two * second[block] + (1.0 - beta_two) * pseudo * pseudo
                lead = (beta_one * moved + (1.0 - beta_one) * pseudo) / (1.0 - beta_one ** (STEP + 1))
                scale = spread / (1.0 - beta_two**STEP)
                value = old - outer_rate * (lead / (jnp.sqrt(scale) + epsilon) + weight_decay * old)
                new_master[block] = value
                new_first[block] = moved
                new_second[block] = spread
                out[dc, h] = value.astype(BF16)


def update(info, parts, master, first, second):
    return call(
        update_kernel,
        "update",
        [jax.ShapeDtypeStruct((10, 14336), F32)] * 3 + [jax.ShapeDtypeStruct((2, 2, 10, 896), BF16)] * 4,
        [SMEM] + [VMEM] * 7,
        [VMEM] * 7,
        (info, *parts, master, first, second),
    )


def split_kernel(info, *refs):
    parts, out = refs[:4], refs[4]
    for dy, part in enumerate(parts):
        out[lax.rem(info[Y] + 4 - dy, 4)] = part[1]


def split(info, parts):
    return call(
        split_kernel,
        "split",
        jax.ShapeDtypeStruct((4, 2, 10, 896), BF16),
        [SMEM] + [VMEM] * 4,
        VMEM,
        (info, *parts),
    )


def weave_kernel(info, *refs):
    parts, other, outs, groups, rows = refs[:4], refs[4], refs[5:7], refs[7], refs[8]
    for dy, part in enumerate(parts):
        y = lax.rem(info[Y] + 4 - dy, 4)
        for h in range(2):
            groups[h, 2 * y + info[CORE]] = part[0, h].astype(F32)
    for y in range(4):
        for h in range(2):
            groups[h, 2 * y + 1 - info[CORE]] = other[y, h].astype(F32)
    for h, out in enumerate(outs):
        for k in range(8):
            rows[h, k * 10 : (k + 1) * 10, :] = groups[h, k]
        out[...] = rows[h].astype(BF16)


def weave(info, parts, other):
    return call(
        weave_kernel,
        "weave",
        [jax.ShapeDtypeStruct((80, 896), BF16)] * 2,
        [SMEM] + [VMEM] * 5,
        [VMEM] * 2,
        (info, *parts, other),
        [pltpu.VMEM((2, 8, 10, 896), F32), pltpu.VMEM((2, 80, 896), F32)],
    )


def merge_kernel(info, *refs):
    parts, out, rows = refs[:4], refs[4], refs[5]
    low = info[ZHI] == 0
    for n in range(2):
        mine, far = parts[2 * n][...].astype(F32), parts[2 * n + 1][...].astype(F32)
        for k, block in enumerate((jnp.where(low, mine, far), jnp.where(low, far, mine))):
            for y in range(4):
                at = n * 160 + y * 40 + k * 20
                rows[at : at + 20, :] = block[y * 20 : (y + 1) * 20, :]
    out[...] = rows[...].astype(BF16)


def merge(info, parts):
    return call(
        merge_kernel,
        "merge",
        jax.ShapeDtypeStruct((320, 896), BF16),
        [SMEM] + [VMEM] * 4,
        VMEM,
        (info, *parts),
        [pltpu.VMEM((320, 896), F32)],
    )


def place_kernel(info, *refs):
    blocks, out, sem = refs[:10], refs[10], refs[11]
    k = 0
    for block in blocks:
        for first in range(0, block.shape[0], 160):
            at = pl.multiple_of(info[PLACE + k], 32)
            pltpu.make_async_copy(
                block.at[pl.ds(first, 160), :], out.at[pl.ds(at, 160), :], sem
            ).start()
            k += 1
    pltpu.make_async_copy(out, out, sem).wait()


def place(info, blocks):
    return call(
        place_kernel,
        "place",
        jax.ShapeDtypeStruct((2560, 896), BF16),
        [SMEM] + [VMEM] * 10,
        ANY,
        (info, *blocks),
        [pltpu.SemaphoreType.DMA],
    )


def tie(*values):
    return lax.optimization_barrier(values)


def on_device(features, cotangent, master, first_moment, second_moment):
    device = lax.axis_index("rep") * 16 + lax.axis_index("tp")
    info = lax.dynamic_index_in_dim(jnp.asarray(facts()), device, 0, keepdims=False)

    own, half_a, half_b = prepare(info, features)
    far_a, far_b = send(half_a, dz=2), send(half_b, dz=-2)
    left, right = send(own, dy=1), send(own, dy=-1)
    own_c = send(own, dc=1)
    far_a, far_b, left, right, own_c = tie(far_a, far_b, left, right, own_c)
    far_a, far_b = send(far_a, dz=2), send(far_b, dz=-2)
    opposite_a, opposite_b = send(left[:1280], dy=1), send(right[1280:], dy=-1)
    left_c = send(left, dc=1)
    g = fetch(info, cotangent, left)
    far_a, far_b, opposite_a, opposite_b, left_c, g, right = tie(
        far_a, far_b, opposite_a, opposite_b, left_c, g, right
    )
    a_left, a_right = send(far_a, dy=1), send(far_a, dy=-1)
    b_left, b_right = send(far_b, dy=1), send(far_b, dy=-1)
    right_c, far_a_c, far_b_c = send(right, dc=1), send(far_a, dc=1), send(far_b, dc=1)
    opposite_a_c, opposite_b_c = send(opposite_a, dc=1), send(opposite_b, dc=1)
    a_left, a_right, b_left, b_right, right_c, far_a_c, far_b_c, opposite_a_c, opposite_b_c = tie(
        a_left, a_right, b_left, b_right, right_c, far_a_c, far_b_c, opposite_a_c, opposite_b_c
    )
    a_far, b_far = send(a_left, dy=1), send(b_right, dy=-1)
    a_left_c, a_right_c = send(a_left, dc=1), send(a_right, dc=1)
    b_left_c, b_right_c = send(b_left, dc=1), send(b_right, dc=1)
    a_far, b_far, a_left_c, a_right_c, b_left_c, b_right_c = tie(
        a_far, b_far, a_left_c, a_right_c, b_left_c, b_right_c
    )
    a_far_c, b_far_c = tie(send(a_far, dc=1), send(b_far, dc=1))

    def around(dx):
        first = 640 * ACROSS.index(dx)
        whole = [(piece, first) for piece in (own, own_c, left, left_c, right, right_c)]
        if first < 1280:
            halves = (
                opposite_a, opposite_a_c, far_a, far_a_c, a_left, a_left_c, a_right, a_right_c, a_far, a_far_c
            )
        else:
            halves = (
                opposite_b, opposite_b_c, far_b, far_b_c, b_left, b_left_c, b_right, b_right_c, b_far, b_far_c
            )
        return whole + [(piece, first % 1280) for piece in halves]

    def add(first, *others):
        total = first.astype(F32)
        for other in others:
            total = total + other.astype(F32)
        return total.astype(BF16)

    def cut(total, chunk):
        result = {}
        for i, (j, h) in enumerate(CHUNKS[chunk]):
            part = total[i * 80 : (i + 1) * 80]
            result[j, h] = part if (j, h) == (0, 0) else send_z(part, j, h)
        return result

    two_ac, two_bd = term_rows(2, info, around(2), g)
    two_ac, two_bd = send(two_ac, dx=1), send(two_bd, dx=-1)
    ahead = term_rows(1, info, around(1), g)
    plain_b = send(ahead[1], dx=1)
    carried_a = add(ahead[0], two_ac[:160])
    behind = term_rows(3, info, around(3), g)
    plain_a = send(behind[0], dx=-1)
    carried_b = add(behind[1], two_bd[:160])
    carried_a, carried_b = send(carried_a, dx=1), send(carried_b, dx=-1)
    plain_d, plain_c, _, _ = tie(ahead[3], behind[2], two_ac, two_bd)
    plain_d, plain_c = send(plain_d, dx=1), send(plain_c, dx=-1)
    here = term_rows(0, info, around(0), g)
    carried_c, carried_d = add(ahead[2], two_ac[160:]), add(behind[3], two_bd[160:])
    sum_a, sum_b = add(here[0], plain_a, carried_a), add(here[1], plain_b, carried_b)
    carried_c, carried_d, sum_a, sum_b = tie(carried_c, carried_d, sum_a, sum_b)
    carried_c, carried_d = send(carried_c, dx=1), send(carried_d, dx=-1)
    parts = {**cut(sum_a, 0), **cut(sum_b, 1)}
    parts.update(cut(add(here[2], plain_c, carried_c), 2))
    parts.update(cut(add(here[3], plain_d, carried_d), 3))

    mine, theirs = collect(info, [parts[j, h] for h in range(2) for j in range(4)])
    packed = pack(info, mine, send(theirs, dc=1))
    packed = [send(part, dy=dy) if dy else part for dy, part in enumerate(packed)]
    new_master, new_first, new_second, *fresh = update(
        info, packed, master, first_moment, second_moment
    )
    fresh = [send(fresh[-dy % 4], dy=dy) if dy else fresh[0] for dy in range(4)]
    same, other = weave(info, fresh, send(split(info, fresh), dc=1))

    block = merge(info, [send_z(value, j, h) for j in PAIRS[0] for h, value in enumerate((same, other))])
    block, same, other = tie(block, same, other)
    left, right = send(block, dx=1), send(block, dx=-1)
    parts = [same, send_z(other, 0, 1), send_z(same, 2, 0), send_z(other, 2, 1)]
    *parts, left, right = tie(*parts, left, right)
    low, high = send(left[:160], dx=1), send(right[160:], dx=-1)
    blocks = [block, left, right, low, high]
    block = merge(info, parts)
    left, right = send(block, dx=1), send(block, dx=-1)
    low, high = send(left[:160], dx=1), send(right[160:], dx=-1)
    blocks += [block, left, right, low, high]
    new_weights = place(info, blocks)
    return (new_master, new_first, new_second, new_weights)


def solution(mesh):
    in_specs = (
        P(("rep", "tp"), None),
        P("rep", "tp"),
        P(("rep", "tp"), None),
        P(("rep", "tp"), None),
        P(("rep", "tp"), None),
    )
    out_specs = (
        P(("rep", "tp"), None),
        P(("rep", "tp"), None),
        P(("rep", "tp"), None),
        P(None, "tp"),
    )
    return jax.shard_map(
        on_device, mesh=mesh, in_specs=in_specs, out_specs=out_specs, check_vma=False
    )
```

```python
import functools

import jax
import jax.numpy as jnp
import numpy as np
from jax import lax
from jax.experimental import pallas as pl
from jax.experimental.pallas import tpu as pltpu
from jax.sharding import PartitionSpec as P

STEP = 10

beta_one = 0.9
beta_two = 0.95
outer_rate = 0.05
weight_decay = 0.1
epsilon = 1e-08

BOTH = ("rep", "tp")
BF16, F32 = jnp.bfloat16, jnp.float32
MIB = 1024 * 1024
SMEM = pl.BlockSpec(memory_space=pltpu.SMEM)
VMEM = pl.BlockSpec(memory_space=pltpu.VMEM)
ANY = pl.BlockSpec(memory_space=pl.ANY)

ACROSS = (2, 1, 3, 0)
CHUNKS = (((0, 1), (0, 0)), ((2, 0), (2, 1)), ((1, 0), (1, 1)), ((3, 0), (3, 1)))
ALONE = ((0,), (1,), (2,), (3,))
CUTS = {2: ((0, 2), (1, 3)), 1: ALONE, 3: ALONE, 0: ALONE}
PIECES = tuple((dy, dh, dc) for dh in range(2) for dy in (0, 3, 1, 2) for dc in range(2))
PAIRS = ((1, 3), (0, 2))


def facts():
    rows = []
    for rep in range(16):
        for tp in range(16):
            x, zlo = rep // 4, rep % 4
            row = [x, zlo, tp // 4, tp // 2 % 2, tp % 2]
            row += [
                ((x + dx) % 4 * 4 + (zlo - j) % 4) * 160 for pair in PAIRS for dx in (0, 3, 1, 2) for j in pair
            ]
            y, zhi, core = row[2:5]
            row += [((y + dy) % 4 * 4 + (zhi ^ dh) * 2 + (core ^ dc)) * 128 for dy, dh, dc in PIECES]
            rows.append(row)
    return np.asarray(rows, np.int32)


X, ZLO, Y, ZHI, CORE, PLACE, TOKEN = 0, 1, 2, 3, 4, 5, 21


def pairs(move):
    def index(x, z, y, c):
        x, z, y, c = x % 4, z % 8, y % 4, c % 2
        return (x * 4 + z % 4) * 16 + y * 4 + (z // 4) * 2 + c

    return [
        (index(x, z, y, c), index(*move(x, z, y, c)))
        for x in range(4)
        for z in range(8)
        for y in range(4)
        for c in range(2)
    ]


def send(value, dx=0, dz=0, dy=0, dc=0):
    return lax.ppermute(value, BOTH, pairs(lambda x, z, y, c: (x + dx, z + dz, y + dy, c + dc)))


def send_z(value, j, h):
    def move(x, z, y, c):
        return x, (z // 4 ^ h) * 4 + (z + j) % 4, y, c

    return lax.ppermute(value, BOTH, pairs(move))


def call(kernel, name, out_shape, in_specs, out_specs, args, scratch=(), limit=16, size=1024):
    return pl.pallas_call(
        kernel,
        out_shape=out_shape,
        in_specs=in_specs,
        out_specs=out_specs,
        scratch_shapes=list(scratch),
        compiler_params=pltpu.CompilerParams(vmem_limit_bytes=limit * MIB),
        cost_estimate=pl.CostEstimate(flops=0, bytes_accessed=size, transcendentals=0),
        name=name,
    )(*args)


def prepare_kernel(info, rows, out, half_a, half_b, turned, ordered):
    for k in range(20):
        turned[k * 128 : (k + 1) * 128, :] = rows[:, k * 128 : (k + 1) * 128].astype(F32).T
    at = 0
    for dx in ACROSS:
        for j in range(4):
            start = lax.rem(info[X] + dx, 4) * 640 + lax.rem(info[ZLO] + j, 4) * 160
            for zhi in range(2):
                for y in range(4):
                    ordered[at : at + 20, :] = turned[pl.ds(start + y * 40 + zhi * 20, 20), :]
                    at += 20
    half_a[...] = ordered[:1280, :].astype(BF16)
    half_b[...] = ordered[1280:, :].astype(BF16)
    out[...] = ordered[...].astype(BF16)


def prepare(info, features):
    return call(
        prepare_kernel,
        "prepare",
        [jax.ShapeDtypeStruct((2560, 128), BF16)] + [jax.ShapeDtypeStruct((1280, 128), BF16)] * 2,
        [SMEM, VMEM],
        [VMEM] * 3,
        (info, features),
        [pltpu.VMEM((2560, 128), F32), pltpu.VMEM((2560, 128), F32)],
    )


def fetch_kernel(info, g, _, out):
    for k in range(16):
        start = pl.multiple_of(info[TOKEN + k], 128)
        out[k * 128 : (k + 1) * 128, :] = g[pl.ds(start, 128), :]


def fetch(info, g, after):
    return call(
        fetch_kernel,
        "fetch",
        jax.ShapeDtypeStruct((2048, 896), BF16),
        [SMEM, VMEM, ANY],
        VMEM,
        (info, g, after),
        size=4 * MIB,
    )


def term_kernel(firsts, cuts, info, *refs):
    pieces, g, outs, total = refs[:16], refs[16], refs[17:-1], refs[-1]
    rows = jnp.concatenate([piece[first : first + 640, :] for piece, first in zip(pieces, firsts)], axis=1)
    for start in range(0, 896, 256):
        stop = min(start + 256, 896)
        total[:, start:stop] = jnp.dot(rows, g[:, start:stop], preferred_element_type=F32)
    for out, cut in zip(outs, cuts):
        for k, (j, h) in enumerate(piece for chunk in cut for piece in CHUNKS[chunk]):
            at = pl.multiple_of(j * 160 + lax.rem(info[ZHI] + h, 2) * 80, 16)
            out[k * 80 : (k + 1) * 80, :] = total[pl.ds(at, 80), :].astype(BF16)


def term_rows(dx, info, pieces, g):
    arrays, firsts = zip(*pieces)
    return call(
        functools.partial(term_kernel, firsts, CUTS[dx]),
        "term_rows",
        [jax.ShapeDtypeStruct((160 * len(cut), 896), BF16) for cut in CUTS[dx]],
        [SMEM] + [VMEM] * 17,
        [VMEM] * len(CUTS[dx]),
        (info, *arrays, g),
        [pltpu.VMEM((640, 896), F32)],
        limit=24,
    )


def collect_kernel(info, *refs):
    parts, mine, theirs, total = refs[:8], refs[8], refs[9], refs[10]
    for h in range(2):
        block = [parts[4 * h + j][...].astype(F32) for j in range(4)]
        block = (block[0] + block[1]) + (block[2] + block[3])
        for k in range(8):
            total[h, k] = block[k * 10 : (k + 1) * 10, :]
    for y in range(4):
        for h in range(2):
            mine[y, h] = total[h, 2 * y + info[CORE]].astype(BF16)
            theirs[y, h] = total[h, 2 * y + 1 - info[CORE]].astype(BF16)


def collect(info, parts):
    return call(
        collect_kernel,
        "collect",
        [jax.ShapeDtypeStruct((4, 2, 10, 896), BF16)] * 2,
        [SMEM] + [VMEM] * 8,
        [VMEM] * 2,
        (info, *parts),
        [pltpu.VMEM((2, 8, 10, 896), F32)],
    )


def pack_kernel(info, mine, other, *outs):
    for dy, out in enumerate(outs):
        y = lax.rem(info[Y] + dy, 4)
        out[0] = mine[y]
        out[1] = other[y]


def pack(info, mine, other):
    return call(
        pack_kernel,
        "pack",
        [jax.ShapeDtypeStruct((2, 2, 10, 896), BF16)] * 4,
        [SMEM] + [VMEM] * 2,
        [VMEM] * 4,
        (info, mine, other),
    )


def update_kernel(info, *refs):
    parts, (master, first, second) = refs[:4], refs[4:7]
    new_master, new_first, new_second = refs[7:10]
    fresh = refs[10:]
    for dy, (part, out) in enumerate(zip(parts, fresh)):
        for dc in range(2):
            for h in range(2):
                column = (
                    lax.rem(info[Y] + 4 - dy, 4) * 4
                    + lax.rem(info[ZHI] + h, 2) * 2
                    + lax.rem(info[CORE] + dc, 2)
                ) * 896
                block = (slice(None), pl.ds(pl.multiple_of(column, 128), 896))
                pseudo = part[dc, h].astype(F32) / 16.0
                old = master[block]
                moved = beta_one * first[block] + (1.0 - beta_one) * pseudo
                spread = beta_two * second[block] + (1.0 - beta_two) * pseudo * pseudo
                lead = (beta_one * moved + (1.0 - beta_one) * pseudo) / (1.0 - beta_one ** (STEP + 1))
                scale = spread / (1.0 - beta_two**STEP)
                value = old - outer_rate * (lead / (jnp.sqrt(scale) + epsilon) + weight_decay * old)
                new_master[block] = value
                new_first[block] = moved
                new_second[block] = spread
                out[dc, h] = value.astype(BF16)


def update(info, parts, master, first, second):
    return call(
        update_kernel,
        "update",
        [jax.ShapeDtypeStruct((10, 14336), F32)] * 3 + [jax.ShapeDtypeStruct((2, 2, 10, 896), BF16)] * 4,
        [SMEM] + [VMEM] * 7,
        [VMEM] * 7,
        (info, *parts, master, first, second),
    )


def split_kernel(info, *refs):
    parts, out = refs[:4], refs[4]
    for dy, part in enumerate(parts):
        out[lax.rem(info[Y] + 4 - dy, 4)] = part[1]


def split(info, parts):
    return call(
        split_kernel,
        "split",
        jax.ShapeDtypeStruct((4, 2, 10, 896), BF16),
        [SMEM] + [VMEM] * 4,
        VMEM,
        (info, *parts),
    )


def weave_kernel(info, *refs):
    parts, other, outs, groups, rows = refs[:4], refs[4], refs[5:7], refs[7], refs[8]
    for dy, part in enumerate(parts):
        y = lax.rem(info[Y] + 4 - dy, 4)
        for h in range(2):
            groups[h, 2 * y + info[CORE]] = part[0, h].astype(F32)
    for y in range(4):
        for h in range(2):
            groups[h, 2 * y + 1 - info[CORE]] = other[y, h].astype(F32)
    for h, out in enumerate(outs):
        for k in range(8):
            rows[h, k * 10 : (k + 1) * 10, :] = groups[h, k]
        out[...] = rows[h].astype(BF16)


def weave(info, parts, other):
    return call(
        weave_kernel,
        "weave",
        [jax.ShapeDtypeStruct((80, 896), BF16)] * 2,
        [SMEM] + [VMEM] * 5,
        [VMEM] * 2,
        (info, *parts, other),
        [pltpu.VMEM((2, 8, 10, 896), F32), pltpu.VMEM((2, 80, 896), F32)],
    )


def merge_kernel(info, *refs):
    parts, out, rows = refs[:4], refs[4], refs[5]
    low = info[ZHI] == 0
    for n in range(2):
        mine, far = parts[2 * n][...].astype(F32), parts[2 * n + 1][...].astype(F32)
        for k, block in enumerate((jnp.where(low, mine, far), jnp.where(low, far, mine))):
            for y in range(4):
                at = n * 160 + y * 40 + k * 20
                rows[at : at + 20, :] = block[y * 20 : (y + 1) * 20, :]
    out[...] = rows[...].astype(BF16)


def merge(info, parts):
    return call(
        merge_kernel,
        "merge",
        jax.ShapeDtypeStruct((320, 896), BF16),
        [SMEM] + [VMEM] * 4,
        VMEM,
        (info, *parts),
        [pltpu.VMEM((320, 896), F32)],
    )


def place_kernel(info, *refs):
    blocks, out, sem = refs[:10], refs[10], refs[11]
    k = 0
    for block in blocks:
        for first in range(0, block.shape[0], 160):
            at = pl.multiple_of(info[PLACE + k], 32)
            pltpu.make_async_copy(
                block.at[pl.ds(first, 160), :], out.at[pl.ds(at, 160), :], sem
            ).start()
            k += 1
    pltpu.make_async_copy(out, out, sem).wait()


def place(info, blocks):
    return call(
        place_kernel,
        "place",
        jax.ShapeDtypeStruct((2560, 896), BF16),
        [SMEM] + [VMEM] * 10,
        ANY,
        (info, *blocks),
        [pltpu.SemaphoreType.DMA],
    )


def tie(*values):
    return lax.optimization_barrier(values)


def on_device(features, cotangent, master, first_moment, second_moment):
    device = lax.axis_index("rep") * 16 + lax.axis_index("tp")
    info = lax.dynamic_index_in_dim(jnp.asarray(facts()), device, 0, keepdims=False)

    own, half_a, half_b = prepare(info, features)
    a_here, left, right, own_c, half_b = tie(
        send(half_a, dz=4), send(own, dy=1), send(own, dy=-1), send(own, dc=1), half_b
    )
    b_here, a_left, a_right = send(half_b, dz=4), send(a_here, dy=1), send(a_here, dy=-1)
    opposite_a, opposite_b = send(left[:1280], dy=1), send(right[1280:], dy=-1)
    g = fetch(info, cotangent, left)
    opposite_a, opposite_b, left, right, a_here, g = tie(opposite_a, opposite_b, left, right, a_here, g)
    left_c, right_c, a_here_c = send(left, dc=1), send(right, dc=1), send(a_here, dc=1)
    b_here, a_left, a_right, left_c, right_c, a_here_c, opposite_a, opposite_b = tie(
        b_here, a_left, a_right, left_c, right_c, a_here_c, opposite_a, opposite_b
    )
    a_two, a_one = send(a_left[:640], dy=1), send(a_right[640:], dy=-1)
    b_left, b_right, b_here_c = send(b_here, dy=1), send(b_here, dy=-1), send(b_here, dc=1)
    a_two, a_one, a_left, a_right, opposite_a, opposite_b, b_here_c = tie(
        a_two, a_one, a_left, a_right, opposite_a, opposite_b, b_here_c
    )
    a_two_c, a_one_c = send(a_two, dc=1), send(a_one, dc=1)
    a_left_c, a_right_c = send(a_left, dc=1), send(a_right, dc=1)
    opposite_a_c, opposite_b_c = send(opposite_a, dc=1), send(opposite_b, dc=1)
    a_two_c, a_one_c, a_left_c, a_right_c, opposite_a_c, opposite_b_c, b_left, b_right = tie(
        a_two_c, a_one_c, a_left_c, a_right_c, opposite_a_c, opposite_b_c, b_left, b_right
    )
    b_three, b_none = send(b_left[:640], dy=1), send(b_right[640:], dy=-1)

    def around(dx, *more):
        first = 640 * ACROSS.index(dx)
        pieces = [own, own_c, left, left_c, right, right_c]
        if first < 1280:
            pieces += [opposite_a, opposite_a_c, a_here, a_here_c, a_left, a_left_c, a_right, a_right_c]
        else:
            pieces += [opposite_b, opposite_b_c, b_here, b_here_c, b_left, b_left_c, b_right, b_right_c]
        return [(piece, first % piece.shape[0]) for piece in pieces + list(more)]

    def add(first, *others):
        total = first.astype(F32)
        for other in others:
            total = total + other.astype(F32)
        return total.astype(BF16)

    def cut(total, chunk):
        result = {}
        for i, (j, h) in enumerate(CHUNKS[chunk]):
            part = total[i * 80 : (i + 1) * 80]
            result[j, h] = part if (j, h) == (0, 0) else send_z(part, j, h)
        return result

    two_ac, two_bd = term_rows(2, info, around(2, a_two, a_two_c), g)
    two_ac, two_bd = tie(send(two_ac, dx=1), send(two_bd, dx=-1))
    ahead = term_rows(1, info, around(1, a_one, a_one_c), g)
    b_left, b_right, b_three, b_none, *ahead = tie(b_left, b_right, b_three, b_none, *ahead)
    plain_b = send(ahead[1], dx=1)
    b_left_c, b_right_c = send(b_left, dc=1), send(b_right, dc=1)
    b_three_c, b_none_c = send(b_three, dc=1), send(b_none, dc=1)
    carried_a = add(ahead[0], two_ac[:160])
    behind = term_rows(3, info, around(3, b_three, b_three_c), g)
    plain_a = send(behind[0], dx=-1)
    carried_b = add(behind[1], two_bd[:160])
    carried_a, carried_b = send(carried_a, dx=1), send(carried_b, dx=-1)
    plain_d, plain_c, _, _ = tie(ahead[3], behind[2], two_ac, two_bd)
    plain_d, plain_c = send(plain_d, dx=1), send(plain_c, dx=-1)
    here = term_rows(0, info, around(0, b_none, b_none_c), g)
    carried_c, carried_d = add(ahead[2], two_ac[160:]), add(behind[3], two_bd[160:])
    sum_a, sum_b = add(here[0], plain_a, carried_a), add(here[1], plain_b, carried_b)
    carried_c, carried_d, sum_a, sum_b = tie(carried_c, carried_d, sum_a, sum_b)
    carried_c, carried_d = send(carried_c, dx=1), send(carried_d, dx=-1)
    parts = {**cut(sum_a, 0), **cut(sum_b, 1)}
    parts.update(cut(add(here[2], plain_c, carried_c), 2))
    parts.update(cut(add(here[3], plain_d, carried_d), 3))

    mine, theirs = collect(info, [parts[j, h] for h in range(2) for j in range(4)])
    packed = pack(info, mine, send(theirs, dc=1))
    packed = [send(part, dy=dy) if dy else part for dy, part in enumerate(packed)]
    new_master, new_first, new_second, *fresh = update(
        info, packed, master, first_moment, second_moment
    )
    fresh = [send(fresh[-dy % 4], dy=dy) if dy else fresh[0] for dy in range(4)]
    same, other = weave(info, fresh, send(split(info, fresh), dc=1))

    block = merge(info, [send_z(value, j, h) for j in PAIRS[0] for h, value in enumerate((same, other))])
    block, same, other = tie(block, same, other)
    left, right = send(block, dx=1), send(block, dx=-1)
    parts = [same, send_z(other, 0, 1), send_z(same, 2, 0), send_z(other, 2, 1)]
    *parts, left, right = tie(*parts, left, right)
    low, high = send(left[:160], dx=1), send(right[160:], dx=-1)
    blocks = [block, left, right, low, high]
    block = merge(info, parts)
    left, right = send(block, dx=1), send(block, dx=-1)
    low, high = send(left[:160], dx=1), send(right[160:], dx=-1)
    blocks += [block, left, right, low, high]
    new_weights = place(info, blocks)
    return (new_master, new_first, new_second, new_weights)


def solution(mesh):
    in_specs = (
        P(("rep", "tp"), None),
        P("rep", "tp"),
        P(("rep", "tp"), None),
        P(("rep", "tp"), None),
        P(("rep", "tp"), None),
    )
    out_specs = (
        P(("rep", "tp"), None),
        P(("rep", "tp"), None),
        P(("rep", "tp"), None),
        P(None, "tp"),
    )
    return jax.shard_map(
        on_device, mesh=mesh, in_specs=in_specs, out_specs=out_specs, check_vma=False
    )
```

```python
import functools

import jax
import jax.numpy as jnp
import numpy as np
from jax import lax
from jax.experimental import pallas as pl
from jax.experimental.pallas import tpu as pltpu
from jax.sharding import PartitionSpec as P

STEP = 10

beta_one = 0.9
beta_two = 0.95
outer_rate = 0.05
weight_decay = 0.1
epsilon = 1e-08

BOTH = ("rep", "tp")
BF16, F32 = jnp.bfloat16, jnp.float32
MIB = 1024 * 1024
SMEM = pl.BlockSpec(memory_space=pltpu.SMEM)
VMEM = pl.BlockSpec(memory_space=pltpu.VMEM)
ANY = pl.BlockSpec(memory_space=pl.ANY)

ACROSS = (2, 1, 3, 0)
ALONG = (0, 2, 1, 3)
ALONE = ((0,), (1,), (2,), (3,))
CUTS = {2: ((0, 2), (1, 3)), 1: ALONE, 3: ALONE, 0: ALONE}
PIECES = tuple((dy, dh, dc) for dh in range(2) for dy in (0, 3, 1, 2) for dc in range(2))
ROUND = tuple(
    (dx, j, first, rows)
    for group in ((0,), (1, 3), (2,))
    for dx in (0, 3, 1, 2)
    for j in group
    for first, rows in (((0, 80), (80, 80)) if dx == 2 and len(group) == 1 else ((0, 160),))
)


def facts():
    result = []
    for rep in range(16):
        for tp in range(16):
            x, zlo = rep // 4, rep % 4
            y, zhi, core = tp // 4, tp // 2 % 2, tp % 2
            row = [x, zlo, y, zhi, core]
            row += [((y + dy) % 4 * 4 + (zhi ^ dh) * 2 + (core ^ dc)) * 128 for dy, dh, dc in PIECES]
            row += [((x + dx) % 4 * 4 + (zlo - j) % 4) * 160 + first for dx, j, first, _ in ROUND]
            result.append(row)
    return np.asarray(result, np.int32)


X, ZLO, Y, ZHI, CORE, TOKEN, PLACE = 0, 1, 2, 3, 4, 5, 21


def pairs(move):
    def index(x, z, y, c):
        x, z, y, c = x % 4, z % 8, y % 4, c % 2
        return (x * 4 + z % 4) * 16 + y * 4 + (z // 4) * 2 + c

    return [
        (index(x, z, y, c), index(*move(x, z, y, c)))
        for x in range(4)
        for z in range(8)
        for y in range(4)
        for c in range(2)
    ]


def send(value, dx=0, dz=0, dy=0, dc=0):
    return lax.ppermute(value, BOTH, pairs(lambda x, z, y, c: (x + dx, z + dz, y + dy, c + dc)))


def send_z(value, j):
    return lax.ppermute(value, BOTH, pairs(lambda x, z, y, c: (x, z // 4 * 4 + (z + j) % 4, y, c)))


def call(kernel, name, out_shape, in_specs, out_specs, args, scratch=(), limit=16, size=1024):
    return pl.pallas_call(
        kernel,
        out_shape=out_shape,
        in_specs=in_specs,
        out_specs=out_specs,
        scratch_shapes=list(scratch),
        compiler_params=pltpu.CompilerParams(vmem_limit_bytes=limit * MIB),
        cost_estimate=pl.CostEstimate(flops=0, bytes_accessed=size, transcendentals=0),
        name=name,
    )(*args)


def prepare_kernel(info, rows, out, half_a, half_b, turned, ordered):
    for k in range(20):
        turned[k * 128 : (k + 1) * 128, :] = rows[:, k * 128 : (k + 1) * 128].astype(F32).T
    for n, dx in enumerate(ACROSS):
        for k, j in enumerate(ALONG):
            start = lax.rem(info[X] + dx, 4) * 640 + lax.rem(info[ZLO] + j, 4) * 160
            at = n * 640 + k * 160
            ordered[at : at + 160, :] = turned[pl.ds(pl.multiple_of(start, 32), 160), :]
    half_a[...] = ordered[:1280, :].astype(BF16)
    half_b[...] = ordered[1280:, :].astype(BF16)
    out[...] = ordered[...].astype(BF16)


def prepare(info, features):
    return call(
        prepare_kernel,
        "prepare",
        [jax.ShapeDtypeStruct((2560, 128), BF16)] + [jax.ShapeDtypeStruct((1280, 128), BF16)] * 2,
        [SMEM, VMEM],
        [VMEM] * 3,
        (info, features),
        [pltpu.VMEM((2560, 128), F32), pltpu.VMEM((2560, 128), F32)],
    )


def fetch_kernel(info, g, _, out):
    for k in range(16):
        start = pl.multiple_of(info[TOKEN + k], 128)
        out[k * 128 : (k + 1) * 128, :] = g[pl.ds(start, 128), :]


def fetch(info, g, after):
    return call(
        fetch_kernel,
        "fetch",
        jax.ShapeDtypeStruct((2048, 896), BF16),
        [SMEM, VMEM, ANY],
        VMEM,
        (info, g, after),
        size=4 * MIB,
    )


def term_kernel(firsts, cuts, info, *refs):
    pieces, g, outs, total = refs[:16], refs[16], refs[17:-1], refs[-1]
    rows = jnp.concatenate([piece[first : first + 640, :] for piece, first in zip(pieces, firsts)], axis=1)
    for start in range(0, 896, 256):
        stop = min(start + 256, 896)
        total[:, start:stop] = jnp.dot(rows, g[:, start:stop], preferred_element_type=F32)
    for out, cut in zip(outs, cuts):
        for k, block in enumerate(cut):
            out[k * 160 : (k + 1) * 160, :] = total[block * 160 : (block + 1) * 160, :].astype(BF16)


def term_rows(dx, info, pieces, g):
    arrays, firsts = zip(*pieces)
    return call(
        functools.partial(term_kernel, firsts, CUTS[dx]),
        "term_rows",
        [jax.ShapeDtypeStruct((160 * len(cut), 896), BF16) for cut in CUTS[dx]],
        [SMEM] + [VMEM] * 17,
        [VMEM] * len(CUTS[dx]),
        (info, *arrays, g),
        [pltpu.VMEM((640, 896), F32)],
        limit=24,
    )


def step(pseudo, old, first, second):
    moved = beta_one * first + (1.0 - beta_one) * pseudo
    spread = beta_two * second + (1.0 - beta_two) * pseudo * pseudo
    lead = (beta_one * moved + (1.0 - beta_one) * pseudo) / (1.0 - beta_one ** (STEP + 1))
    scale = spread / (1.0 - beta_two**STEP)
    value = old - outer_rate * (lead / (jnp.sqrt(scale) + epsilon) + weight_decay * old)
    return value, moved, spread


def columns(info, y, flip, core):
    at = (y * 4 + lax.rem(info[ZHI] + flip, 2) * 2 + core) * 896
    return (slice(None), pl.ds(pl.multiple_of(at, 128), 896))


def state_kernel(info, master, first, second, near, far_a, far_b, rows):
    for flip, (low, high) in enumerate(((near.at[0:2], near.at[2:4]), (far_a, far_b))):
        for y in range(4):
            for core in range(2):
                block = columns(info, y, flip, core)
                old = master[block]
                top = old.astype(BF16).astype(F32)
                rows[0:10, :] = top
                rows[10:20, :] = old - top
                rows[20:30, :] = first[block]
                rows[30:40, :] = second[block]
                (low if y < 2 else high)[y % 2, core] = rows[...].astype(BF16)


def state(info, master, first, second):
    return call(
        state_kernel,
        "state",
        [jax.ShapeDtypeStruct((4, 2, 40, 896), BF16)] + [jax.ShapeDtypeStruct((2, 2, 40, 896), BF16)] * 2,
        [SMEM] + [VMEM] * 3,
        [VMEM] * 3,
        (info, master, first, second),
        [pltpu.VMEM((40, 896), F32)],
    )


def state_y_kernel(info, near, far_a, far_b, *refs):
    outs, far = refs[:4], refs[4]
    far[0:2] = far_a[...]
    far[2:4] = far_b[...]
    for dy, out in enumerate(outs):
        y = lax.rem(info[Y] + dy, 4)
        out[0] = near[y]
        out[1] = far[y]


def state_y(info, near, far_a, far_b):
    return call(
        state_y_kernel,
        "state_y",
        [jax.ShapeDtypeStruct((2, 2, 40, 896), BF16)] * 4,
        [SMEM] + [VMEM] * 3,
        [VMEM] * 4,
        (info, near, far_a, far_b),
        [pltpu.VMEM((4, 2, 40, 896), BF16)],
    )


def state_core_kernel(info, *refs):
    parts, out = refs[:4], refs[4]
    for dy, part in enumerate(parts):
        y = lax.rem(info[Y] + 4 - dy, 4)
        for flip in range(2):
            out[y, flip] = part[flip, 1 - info[CORE]]


def state_core(info, parts):
    return call(
        state_core_kernel,
        "state_core",
        jax.ShapeDtypeStruct((4, 2, 40, 896), BF16),
        [SMEM] + [VMEM] * 4,
        VMEM,
        (info, *parts),
    )


def arrange_kernel(info, *refs):
    parts, other, out = refs[:4], refs[4], refs[5]
    core = info[CORE]
    for dy, part in enumerate(parts):
        y = lax.rem(info[Y] + 4 - dy, 4)
        for flip in range(2):
            at = y * 4 + lax.rem(info[ZHI] + flip, 2) * 2
            out[at + core] = part[flip, core]
            out[at + 1 - core] = other[y, flip]


def arrange(info, parts, other):
    return call(
        arrange_kernel,
        "arrange",
        jax.ShapeDtypeStruct((16, 40, 896), BF16),
        [SMEM] + [VMEM] * 5,
        VMEM,
        (info, *parts, other),
    )


def weights_kernel(info, *refs):
    parts, held, out, mine, theirs, rows, groups = refs[:4], refs[4], refs[5], refs[6], refs[7], refs[8], refs[9]
    block = [part[...].astype(F32) for part in parts]
    total = (block[0] + block[1]) + (block[2] + block[3])
    for k in range(16):
        gradient = total[k * 10 : (k + 1) * 10, :]
        groups[k] = gradient
        kept = held[k].astype(F32)
        value, _, _ = step(gradient / 16.0, kept[0:10, :] + kept[10:20, :], kept[20:30, :], kept[30:40, :])
        rows[k * 10 : (k + 1) * 10, :] = value
    out[...] = rows[...].astype(BF16)
    for y in range(4):
        for zhi in range(2):
            mine[y, zhi] = groups[y * 4 + zhi * 2 + info[CORE]].astype(BF16)
            theirs[y, zhi] = groups[y * 4 + zhi * 2 + 1 - info[CORE]].astype(BF16)


def weights(info, parts, held):
    return call(
        weights_kernel,
        "weights",
        [jax.ShapeDtypeStruct((160, 896), BF16)] + [jax.ShapeDtypeStruct((4, 2, 10, 896), BF16)] * 2,
        [SMEM] + [VMEM] * 5,
        [VMEM] * 3,
        (info, *parts, held),
        [pltpu.VMEM((160, 896), F32), pltpu.VMEM((16, 10, 896), F32)],
    )


def pack_kernel(info, mine, other, *outs):
    for dy, out in enumerate(outs):
        y = lax.rem(info[Y] + dy, 4)
        out[0] = mine[y]
        out[1] = other[y]


def pack(info, mine, other):
    return call(
        pack_kernel,
        "pack",
        [jax.ShapeDtypeStruct((2, 2, 10, 896), BF16)] * 4,
        [SMEM] + [VMEM] * 2,
        [VMEM] * 4,
        (info, mine, other),
    )


def flip_kernel(info, *refs):
    parts, out = refs[:4], refs[4]
    for dy, part in enumerate(parts):
        for dc in range(2):
            out[lax.rem(info[Y] + 4 - dy, 4), dc] = part[dc, 1 - info[ZHI]]


def flip(info, parts):
    return call(
        flip_kernel,
        "flip",
        jax.ShapeDtypeStruct((4, 2, 10, 896), BF16),
        [SMEM] + [VMEM] * 4,
        VMEM,
        (info, *parts),
    )


def update_kernel(info, *refs):
    parts, far, (master, first, second) = refs[:4], refs[4], refs[5:8]
    new_master, new_first, new_second = refs[8:]
    for dy, part in enumerate(parts):
        y = lax.rem(info[Y] + 4 - dy, 4)
        for dc in range(2):
            core = lax.rem(info[CORE] + dc, 2)
            for other in range(2):
                block = columns(info, y, other, core)
                gradient = far[y, dc] if other else part[dc, info[ZHI]]
                value, moved, spread = step(
                    gradient.astype(F32) / 16.0, master[block], first[block], second[block]
                )
                new_master[block] = value
                new_first[block] = moved
                new_second[block] = spread


def update(info, parts, far, master, first, second):
    return call(
        update_kernel,
        "update",
        [jax.ShapeDtypeStruct((10, 14336), F32)] * 3,
        [SMEM] + [VMEM] * 8,
        [VMEM] * 3,
        (info, *parts, far, master, first, second),
    )


def place_kernel(info, *refs):
    blocks, out, sem = refs[:-2], refs[-2], refs[-1]
    spans = iter(enumerate(ROUND))
    for block in blocks:
        first = 0
        while first < block.shape[0]:
            k, (_, _, _, rows) = next(spans)
            at = pl.multiple_of(info[PLACE + k], 16)
            pltpu.make_async_copy(
                block.at[pl.ds(first, rows), :], out.at[pl.ds(at, rows), :], sem
            ).start()
            first += rows
    pltpu.make_async_copy(out, out, sem).wait()


def place(info, blocks):
    return call(
        place_kernel,
        "place",
        jax.ShapeDtypeStruct((2560, 896), BF16),
        [SMEM] + [VMEM] * len(blocks),
        ANY,
        (info, *blocks),
        [pltpu.SemaphoreType.DMA],
    )


def tie(*values):
    return lax.optimization_barrier(values)


def on_device(features, cotangent, master, first_moment, second_moment):
    device = lax.axis_index("rep") * 16 + lax.axis_index("tp")
    info = lax.dynamic_index_in_dim(jnp.asarray(facts()), device, 0, keepdims=False)

    own, half_a, half_b = prepare(info, features)
    near, far_a, far_b = state(info, master, first_moment, second_moment)
    a_here, left, right, own_c, half_b = tie(
        send(half_a, dz=4), send(own, dy=1), send(own, dy=-1), send(own, dc=1), half_b
    )
    b_here, a_left, a_right = send(half_b, dz=4), send(a_here, dy=1), send(a_here, dy=-1)
    opposite_a, opposite_b = send(left[:1280], dy=1), send(right[1280:], dy=-1)
    g = fetch(info, cotangent, left)
    opposite_a, opposite_b, left, right, a_here, g = tie(opposite_a, opposite_b, left, right, a_here, g)
    left_c, right_c, a_here_c = send(left, dc=1), send(right, dc=1), send(a_here, dc=1)
    b_here, a_left, a_right, left_c, right_c, a_here_c, opposite_a, opposite_b, far_a, far_b = tie(
        b_here, a_left, a_right, left_c, right_c, a_here_c, opposite_a, opposite_b, far_a, far_b
    )
    far_a = send(far_a, dz=4)
    a_two, a_one = send(a_left[:640], dy=1), send(a_right[640:], dy=-1)
    b_left, b_right = send(b_here, dy=1), send(b_here, dy=-1)
    a_two, a_one, a_left, a_right, opposite_a, opposite_b, b_here, far_a = tie(
        a_two, a_one, a_left, a_right, opposite_a, opposite_b, b_here, far_a
    )
    b_here_c = send(b_here, dc=1)
    a_two_c, a_one_c = send(a_two, dc=1), send(a_one, dc=1)
    a_left_c, a_right_c = send(a_left, dc=1), send(a_right, dc=1)
    opposite_a_c, opposite_b_c = send(opposite_a, dc=1), send(opposite_b, dc=1)
    a_two_c, a_one_c, a_left_c, a_right_c, opposite_a_c, opposite_b_c, b_left, b_right, b_here_c = tie(
        a_two_c, a_one_c, a_left_c, a_right_c, opposite_a_c, opposite_b_c, b_left, b_right, b_here_c
    )
    b_three, b_none = send(b_left[:640], dy=1), send(b_right[640:], dy=-1)

    def around(dx, *more):
        first = 640 * ACROSS.index(dx)
        pieces = [own, own_c, left, left_c, right, right_c]
        if first < 1280:
            pieces += [opposite_a, opposite_a_c, a_here, a_here_c, a_left, a_left_c, a_right, a_right_c]
        else:
            pieces += [opposite_b, opposite_b_c, b_here, b_here_c, b_left, b_left_c, b_right, b_right_c]
        return [(piece, first % piece.shape[0]) for piece in pieces + list(more)]

    def add(first, *others):
        total = first.astype(F32)
        for other in others:
            total = total + other.astype(F32)
        return total.astype(BF16)

    two_ac, two_bd = term_rows(2, info, around(2, a_two, a_two_c), g)
    two_ac, two_bd, far_b = tie(two_ac, two_bd, far_b)
    two_ac, two_bd, far_b, near, far_a = tie(
        send(two_ac, dx=1), send(two_bd, dx=-1), send(far_b, dz=4), near, far_a
    )
    held = [send(part, dy=dy) if dy else part for dy, part in enumerate(state_y(info, near, far_a, far_b))]
    ahead = term_rows(1, info, around(1, a_one, a_one_c), g)
    b_left, b_right, b_three, b_none, *ahead = tie(b_left, b_right, b_three, b_none, *ahead)
    plain_b = send(ahead[1], dx=1)
    b_left_c, b_right_c = send(b_left, dc=1), send(b_right, dc=1)
    b_three_c, b_none_c = send(b_three, dc=1), send(b_none, dc=1)
    carried_a = add(ahead[0], two_ac[:160])
    behind = term_rows(3, info, around(3, b_three, b_three_c), g)
    plain_a = send(behind[0], dx=-1)
    carried_b = add(behind[1], two_bd[:160])
    carried_a, carried_b = send(carried_a, dx=1), send(carried_b, dx=-1)
    plain_d, plain_c, _, _ = tie(ahead[3], behind[2], two_ac, two_bd)
    plain_d, plain_c = send(plain_d, dx=1), send(plain_c, dx=-1)
    here = term_rows(0, info, around(0, b_none, b_none_c), g)
    carried_c, carried_d = add(ahead[2], two_ac[160:]), add(behind[3], two_bd[160:])
    sum_a, sum_b = add(here[0], plain_a, carried_a), add(here[1], plain_b, carried_b)
    carried_c, carried_d, sum_a, sum_b = tie(carried_c, carried_d, sum_a, sum_b)
    carried_c, carried_d = send(carried_c, dx=1), send(carried_d, dx=-1)
    part_b = send_z(sum_b, 2)
    sum_c, sum_d, part_b, *held = tie(
        add(here[2], plain_c, carried_c), add(here[3], plain_d, carried_d), part_b, *held
    )
    parts = [sum_a, part_b, send_z(sum_c, 1), send_z(sum_d, 3)]
    held = arrange(info, held, send(state_core(info, held), dc=1))
    fresh, mine, theirs = weights(info, parts, held)

    fresh_one, fresh_three, left, right, theirs = tie(
        send_z(fresh, 1), send_z(fresh, 3), send(fresh, dx=1), send(fresh, dx=-1), send(theirs, dc=1)
    )
    low, high = send(left[:80], dx=1), send(right[80:], dx=-1)
    pair, fresh_two = jnp.concatenate([fresh_one, fresh_three], axis=0), send_z(fresh, 2)
    pair_left, pair_right = send(pair, dx=1), send(pair, dx=-1)
    low, high, mine, theirs = tie(low, high, mine, theirs)
    blocks = [fresh, left, right, low, high]
    packed = [send(part, dy=dy) if dy else part for dy, part in enumerate(pack(info, mine, theirs))]
    left, right, fresh_two, *packed = tie(pair_left, pair_right, fresh_two, *packed)
    blocks += [pair, left, right]
    left, right, low, high, far = tie(
        send(fresh_two, dx=1),
        send(fresh_two, dx=-1),
        send(left[:160], dx=1),
        send(right[160:], dx=-1),
        send(flip(info, packed), dz=4),
    )
    blocks += [low, high, fresh_two, left, right, send(left[:80], dx=1), send(right[80:], dx=-1)]
    new_master, new_first, new_second = update(info, packed, far, master, first_moment, second_moment)
    new_weights = place(info, blocks)
    return (new_master, new_first, new_second, new_weights)


def solution(mesh):
    in_specs = (
        P(("rep", "tp"), None),
        P("rep", "tp"),
        P(("rep", "tp"), None),
        P(("rep", "tp"), None),
        P(("rep", "tp"), None),
    )
    out_specs = (
        P(("rep", "tp"), None),
        P(("rep", "tp"), None),
        P(("rep", "tp"), None),
        P(None, "tp"),
    )
    return jax.shard_map(
        on_device, mesh=mesh, in_specs=in_specs, out_specs=out_specs, check_vma=False
    )
```

```python
import functools

import jax
import jax.numpy as jnp
import numpy as np
from jax import lax
from jax.experimental import pallas as pl
from jax.experimental.pallas import tpu as pltpu
from jax.sharding import PartitionSpec as P

STEP = 10

beta_one = 0.9
beta_two = 0.95
outer_rate = 0.05
weight_decay = 0.1
epsilon = 1e-08

BOTH = ("rep", "tp")
BF16, F32 = jnp.bfloat16, jnp.float32
MIB = 1024 * 1024
SMEM = pl.BlockSpec(memory_space=pltpu.SMEM)
VMEM = pl.BlockSpec(memory_space=pltpu.VMEM)
ANY = pl.BlockSpec(memory_space=pl.ANY)

ACROSS = (2, 1, 3, 0)
CHUNKS = (((0, 1), (0, 0)), ((2, 0), (2, 1)), ((1, 0), (1, 1)), ((3, 0), (3, 1)))
ALONE = ((0,), (1,), (2,), (3,))
CUTS = {2: ((0, 2), (1, 3)), 1: ALONE, 3: ALONE, 0: ALONE}
PIECES = tuple((dy, dh, dc) for dh in range(2) for dy in (0, 3, 1, 2) for dc in range(2))
PAIRS = ((1, 3), (0, 2))


def facts():
    rows = []
    for rep in range(16):
        for tp in range(16):
            x, zlo = rep // 4, rep % 4
            row = [x, zlo, tp // 4, tp // 2 % 2, tp % 2]
            row += [
                ((x + dx) % 4 * 4 + (zlo - j) % 4) * 160 for pair in PAIRS for dx in (0, 3, 1, 2) for j in pair
            ]
            y, zhi, core = row[2:5]
            row += [((y + dy) % 4 * 4 + (zhi ^ dh) * 2 + (core ^ dc)) * 128 for dy, dh, dc in PIECES]
            rows.append(row)
    return np.asarray(rows, np.int32)


X, ZLO, Y, ZHI, CORE, PLACE, TOKEN = 0, 1, 2, 3, 4, 5, 21


def pairs(move):
    def index(x, z, y, c):
        x, z, y, c = x % 4, z % 8, y % 4, c % 2
        return (x * 4 + z % 4) * 16 + y * 4 + (z // 4) * 2 + c

    return [
        (index(x, z, y, c), index(*move(x, z, y, c)))
        for x in range(4)
        for z in range(8)
        for y in range(4)
        for c in range(2)
    ]


def send(value, dx=0, dz=0, dy=0, dc=0):
    return lax.ppermute(value, BOTH, pairs(lambda x, z, y, c: (x + dx, z + dz, y + dy, c + dc)))


def send_z(value, j, h):
    def move(x, z, y, c):
        return x, (z // 4 ^ h) * 4 + (z + j) % 4, y, c

    return lax.ppermute(value, BOTH, pairs(move))


def call(kernel, name, out_shape, in_specs, out_specs, args, scratch=(), limit=16, size=1024):
    return pl.pallas_call(
        kernel,
        out_shape=out_shape,
        in_specs=in_specs,
        out_specs=out_specs,
        scratch_shapes=list(scratch),
        compiler_params=pltpu.CompilerParams(vmem_limit_bytes=limit * MIB),
        cost_estimate=pl.CostEstimate(flops=0, bytes_accessed=size, transcendentals=0),
        name=name,
    )(*args)


def prepare_kernel(info, rows, out, half_a, half_b, turned, ordered):
    for k in range(20):
        turned[k * 128 : (k + 1) * 128, :] = rows[:, k * 128 : (k + 1) * 128].astype(F32).T
    at = 0
    for dx in ACROSS:
        for j in range(4):
            start = lax.rem(info[X] + dx, 4) * 640 + lax.rem(info[ZLO] + j, 4) * 160
            for zhi in range(2):
                for y in range(4):
                    ordered[at : at + 20, :] = turned[pl.ds(start + y * 40 + zhi * 20, 20), :]
                    at += 20
    half_a[...] = ordered[:1280, :].astype(BF16)
    half_b[...] = ordered[1280:, :].astype(BF16)
    out[...] = ordered[...].astype(BF16)


def prepare(info, features):
    return call(
        prepare_kernel,
        "prepare",
        [jax.ShapeDtypeStruct((2560, 128), BF16)] + [jax.ShapeDtypeStruct((1280, 128), BF16)] * 2,
        [SMEM, VMEM],
        [VMEM] * 3,
        (info, features),
        [pltpu.VMEM((2560, 128), F32), pltpu.VMEM((2560, 128), F32)],
    )


def fetch_kernel(info, g, _, out):
    for k in range(16):
        start = pl.multiple_of(info[TOKEN + k], 128)
        out[k * 128 : (k + 1) * 128, :] = g[pl.ds(start, 128), :]


def fetch(info, g, after):
    return call(
        fetch_kernel,
        "fetch",
        jax.ShapeDtypeStruct((2048, 896), BF16),
        [SMEM, VMEM, ANY],
        VMEM,
        (info, g, after),
        size=4 * MIB,
    )


def term_kernel(firsts, cuts, info, *refs):
    pieces, g, outs, total = refs[:16], refs[16], refs[17:-1], refs[-1]
    rows = jnp.concatenate([piece[first : first + 640, :] for piece, first in zip(pieces, firsts)], axis=1)
    for start in range(0, 896, 256):
        stop = min(start + 256, 896)
        total[:, start:stop] = jnp.dot(rows, g[:, start:stop], preferred_element_type=F32)
    for out, cut in zip(outs, cuts):
        for k, (j, h) in enumerate(piece for chunk in cut for piece in CHUNKS[chunk]):
            at = pl.multiple_of(j * 160 + lax.rem(info[ZHI] + h, 2) * 80, 16)
            out[k * 80 : (k + 1) * 80, :] = total[pl.ds(at, 80), :].astype(BF16)


def term_rows(dx, info, pieces, g):
    arrays, firsts = zip(*pieces)
    return call(
        functools.partial(term_kernel, firsts, CUTS[dx]),
        "term_rows",
        [jax.ShapeDtypeStruct((160 * len(cut), 896), BF16) for cut in CUTS[dx]],
        [SMEM] + [VMEM] * 17,
        [VMEM] * len(CUTS[dx]),
        (info, *arrays, g),
        [pltpu.VMEM((640, 896), F32)],
        limit=24,
    )


def step(pseudo, old, first, second):
    moved = beta_one * first + (1.0 - beta_one) * pseudo
    spread = beta_two * second + (1.0 - beta_two) * pseudo * pseudo
    lead = (beta_one * moved + (1.0 - beta_one) * pseudo) / (1.0 - beta_one ** (STEP + 1))
    scale = spread / (1.0 - beta_two**STEP)
    value = old - outer_rate * (lead / (jnp.sqrt(scale) + epsilon) + weight_decay * old)
    return value, moved, spread


def columns(info, dy, flip, core):
    at = (lax.rem(info[Y] + 4 + dy, 4) * 4 + lax.rem(info[ZHI] + flip, 2) * 2 + core) * 896
    return (slice(None), pl.ds(pl.multiple_of(at, 128), 896))


def state_kernel(info, master, first, second, *refs):
    outs, rows = refs[:4], refs[4]
    for dy, out in enumerate(outs):
        for core in range(2):
            for flip in range(2):
                block = columns(info, dy, flip, core)
                old = master[block]
                top = old.astype(BF16).astype(F32)
                rows[0:10, :] = top
                rows[10:20, :] = old - top
                rows[20:30, :] = first[block]
                rows[30:40, :] = second[block]
                out[core, flip] = rows[...].astype(BF16)


def state(info, master, first, second):
    return call(
        state_kernel,
        "state",
        [jax.ShapeDtypeStruct((2, 2, 40, 896), BF16)] * 4,
        [SMEM] + [VMEM] * 3,
        [VMEM] * 4,
        (info, master, first, second),
        [pltpu.VMEM((40, 896), F32)],
    )


def state_core_kernel(info, *refs):
    parts, out = refs[:4], refs[4]
    for dy, part in enumerate(parts):
        out[lax.rem(info[Y] + 4 - dy, 4)] = part[1 - info[CORE]]


def state_core(info, parts):
    return call(
        state_core_kernel,
        "state_core",
        jax.ShapeDtypeStruct((4, 2, 40, 896), BF16),
        [SMEM] + [VMEM] * 4,
        VMEM,
        (info, *parts),
    )


def arrange_kernel(info, *refs):
    parts, other, out = refs[:4], refs[4], refs[5]
    core = info[CORE]
    for dy, part in enumerate(parts):
        at = lax.rem(info[Y] + 4 - dy, 4) * 2
        for flip in range(2):
            out[flip, at + core] = part[core, flip]
    for y in range(4):
        for flip in range(2):
            out[flip, 2 * y + 1 - core] = other[y, flip]


def arrange(info, parts, other):
    return call(
        arrange_kernel,
        "arrange",
        jax.ShapeDtypeStruct((2, 8, 40, 896), BF16),
        [SMEM] + [VMEM] * 5,
        VMEM,
        (info, *parts, other),
    )


def weights_kernel(info, *refs):
    parts, held, outs, mine, theirs, rows, groups = refs[:8], refs[8], refs[9:11], refs[11], refs[12], refs[13], refs[14]
    for h, out in enumerate(outs):
        block = [parts[4 * h + j][...].astype(F32) for j in range(4)]
        total = (block[0] + block[1]) + (block[2] + block[3])
        for k in range(8):
            gradient = total[k * 10 : (k + 1) * 10, :]
            groups[h, k] = gradient
            kept = held[h, k].astype(F32)
            value, _, _ = step(gradient / 16.0, kept[0:10, :] + kept[10:20, :], kept[20:30, :], kept[30:40, :])
            rows[k * 10 : (k + 1) * 10, :] = value
        out[...] = rows[...].astype(BF16)
    for y in range(4):
        for h in range(2):
            mine[y, h] = groups[h, 2 * y + info[CORE]].astype(BF16)
            theirs[y, h] = groups[h, 2 * y + 1 - info[CORE]].astype(BF16)


def weights(info, parts, held):
    return call(
        weights_kernel,
        "weights",
        [jax.ShapeDtypeStruct((80, 896), BF16)] * 2 + [jax.ShapeDtypeStruct((4, 2, 10, 896), BF16)] * 2,
        [SMEM] + [VMEM] * 9,
        [VMEM] * 4,
        (info, *parts, held),
        [pltpu.VMEM((80, 896), F32), pltpu.VMEM((2, 8, 10, 896), F32)],
    )


def pack_kernel(info, mine, other, *outs):
    for dy, out in enumerate(outs):
        y = lax.rem(info[Y] + dy, 4)
        out[0] = mine[y]
        out[1] = other[y]


def pack(info, mine, other):
    return call(
        pack_kernel,
        "pack",
        [jax.ShapeDtypeStruct((2, 2, 10, 896), BF16)] * 4,
        [SMEM] + [VMEM] * 2,
        [VMEM] * 4,
        (info, mine, other),
    )


def update_kernel(info, *refs):
    parts, (master, first, second) = refs[:4], refs[4:7]
    new_master, new_first, new_second = refs[7:]
    for dy, part in enumerate(parts):
        for dc in range(2):
            for flip in range(2):
                block = columns(info, -dy, flip, lax.rem(info[CORE] + dc, 2))
                value, moved, spread = step(
                    part[dc, flip].astype(F32) / 16.0, master[block], first[block], second[block]
                )
                new_master[block] = value
                new_first[block] = moved
                new_second[block] = spread


def update(info, parts, master, first, second):
    return call(
        update_kernel,
        "update",
        [jax.ShapeDtypeStruct((10, 14336), F32)] * 3,
        [SMEM] + [VMEM] * 7,
        [VMEM] * 3,
        (info, *parts, master, first, second),
    )


def merge_kernel(info, *refs):
    parts, out, rows = refs[:4], refs[4], refs[5]
    low = info[ZHI] == 0
    for n in range(2):
        mine, far = parts[2 * n][...].astype(F32), parts[2 * n + 1][...].astype(F32)
        for k, block in enumerate((jnp.where(low, mine, far), jnp.where(low, far, mine))):
            for y in range(4):
                at = n * 160 + y * 40 + k * 20
                rows[at : at + 20, :] = block[y * 20 : (y + 1) * 20, :]
    out[...] = rows[...].astype(BF16)


def merge(info, parts):
    return call(
        merge_kernel,
        "merge",
        jax.ShapeDtypeStruct((320, 896), BF16),
        [SMEM] + [VMEM] * 4,
        VMEM,
        (info, *parts),
        [pltpu.VMEM((320, 896), F32)],
    )


def place_kernel(info, *refs):
    blocks, out, sem = refs[:10], refs[10], refs[11]
    k = 0
    for block in blocks:
        for first in range(0, block.shape[0], 160):
            at = pl.multiple_of(info[PLACE + k], 32)
            pltpu.make_async_copy(
                block.at[pl.ds(first, 160), :], out.at[pl.ds(at, 160), :], sem
            ).start()
            k += 1
    pltpu.make_async_copy(out, out, sem).wait()


def place(info, blocks):
    return call(
        place_kernel,
        "place",
        jax.ShapeDtypeStruct((2560, 896), BF16),
        [SMEM] + [VMEM] * 10,
        ANY,
        (info, *blocks),
        [pltpu.SemaphoreType.DMA],
    )


def tie(*values):
    return lax.optimization_barrier(values)


def on_device(features, cotangent, master, first_moment, second_moment):
    device = lax.axis_index("rep") * 16 + lax.axis_index("tp")
    info = lax.dynamic_index_in_dim(jnp.asarray(facts()), device, 0, keepdims=False)

    own, half_a, half_b = prepare(info, features)
    a_here, left, right, own_c, half_b = tie(
        send(half_a, dz=4), send(own, dy=1), send(own, dy=-1), send(own, dc=1), half_b
    )
    b_here, a_left, a_right = send(half_b, dz=4), send(a_here, dy=1), send(a_here, dy=-1)
    opposite_a, opposite_b = send(left[:1280], dy=1), send(right[1280:], dy=-1)
    g = fetch(info, cotangent, left)
    opposite_a, opposite_b, left, right, a_here, g = tie(opposite_a, opposite_b, left, right, a_here, g)
    left_c, right_c, a_here_c = send(left, dc=1), send(right, dc=1), send(a_here, dc=1)
    b_here, a_left, a_right, left_c, right_c, a_here_c, opposite_a, opposite_b = tie(
        b_here, a_left, a_right, left_c, right_c, a_here_c, opposite_a, opposite_b
    )
    a_two, a_one = send(a_left[:640], dy=1), send(a_right[640:], dy=-1)
    b_left, b_right, b_here_c = send(b_here, dy=1), send(b_here, dy=-1), send(b_here, dc=1)
    a_two, a_one, a_left, a_right, opposite_a, opposite_b, b_here_c = tie(
        a_two, a_one, a_left, a_right, opposite_a, opposite_b, b_here_c
    )
    a_two_c, a_one_c = send(a_two, dc=1), send(a_one, dc=1)
    a_left_c, a_right_c = send(a_left, dc=1), send(a_right, dc=1)
    opposite_a_c, opposite_b_c = send(opposite_a, dc=1), send(opposite_b, dc=1)
    a_two_c, a_one_c, a_left_c, a_right_c, opposite_a_c, opposite_b_c, b_left, b_right = tie(
        a_two_c, a_one_c, a_left_c, a_right_c, opposite_a_c, opposite_b_c, b_left, b_right
    )
    b_three, b_none = send(b_left[:640], dy=1), send(b_right[640:], dy=-1)

    def around(dx, *more):
        first = 640 * ACROSS.index(dx)
        pieces = [own, own_c, left, left_c, right, right_c]
        if first < 1280:
            pieces += [opposite_a, opposite_a_c, a_here, a_here_c, a_left, a_left_c, a_right, a_right_c]
        else:
            pieces += [opposite_b, opposite_b_c, b_here, b_here_c, b_left, b_left_c, b_right, b_right_c]
        return [(piece, first % piece.shape[0]) for piece in pieces + list(more)]

    def add(first, *others):
        total = first.astype(F32)
        for other in others:
            total = total + other.astype(F32)
        return total.astype(BF16)

    def cut(total, chunk):
        result = {}
        for i, (j, h) in enumerate(CHUNKS[chunk]):
            part = total[i * 80 : (i + 1) * 80]
            result[j, h] = part if (j, h) == (0, 0) else send_z(part, j, h)
        return result

    two_ac, two_bd = term_rows(2, info, around(2, a_two, a_two_c), g)
    two_ac, two_bd = tie(send(two_ac, dx=1), send(two_bd, dx=-1))
    ahead = term_rows(1, info, around(1, a_one, a_one_c), g)
    b_left, b_right, b_three, b_none, *ahead = tie(b_left, b_right, b_three, b_none, *ahead)
    plain_b = send(ahead[1], dx=1)
    b_left_c, b_right_c = send(b_left, dc=1), send(b_right, dc=1)
    b_three_c, b_none_c = send(b_three, dc=1), send(b_none, dc=1)
    carried_a = add(ahead[0], two_ac[:160])
    behind = term_rows(3, info, around(3, b_three, b_three_c), g)
    plain_a = send(behind[0], dx=-1)
    carried_b = add(behind[1], two_bd[:160])
    carried_a, carried_b = send(carried_a, dx=1), send(carried_b, dx=-1)
    held = list(state(info, master, first_moment, second_moment))
    held[2], two_ac, two_bd = tie(held[2], two_ac, two_bd)
    held[2] = send(held[2], dy=2)
    plain_d, plain_c, _, _ = tie(ahead[3], behind[2], two_ac, two_bd)
    plain_d, plain_c = send(plain_d, dx=1), send(plain_c, dx=-1)
    here = term_rows(0, info, around(0, b_none, b_none_c), g)
    carried_c, carried_d = add(ahead[2], two_ac[160:]), add(behind[3], two_bd[160:])
    sum_a, sum_b = add(here[0], plain_a, carried_a), add(here[1], plain_b, carried_b)
    carried_c, carried_d, sum_a, sum_b, *held = tie(carried_c, carried_d, sum_a, sum_b, *held)
    held[1], held[3] = send(held[1], dy=1), send(held[3], dy=3)
    carried_c, carried_d = send(carried_c, dx=1), send(carried_d, dx=-1)
    parts = {**cut(sum_a, 0), **cut(sum_b, 1)}
    sum_c, sum_d, parts[0, 1], parts[2, 0], parts[2, 1], *held = tie(
        add(here[2], plain_c, carried_c),
        add(here[3], plain_d, carried_d),
        parts[0, 1],
        parts[2, 0],
        parts[2, 1],
        *held,
    )
    parts.update({**cut(sum_c, 2), **cut(sum_d, 3)})
    held = arrange(info, held, send(state_core(info, held), dc=1))
    same, other, mine, theirs = weights(info, [parts[j, h] for h in range(2) for j in range(4)], held)

    theirs = send(theirs, dc=1)
    block = merge(info, [send_z(value, j, h) for j in PAIRS[0] for h, value in enumerate((same, other))])
    block, same, other, mine, theirs = tie(block, same, other, mine, theirs)
    packed = list(pack(info, mine, theirs))
    left, right = send(block, dx=1), send(block, dx=-1)
    parts = [same, send_z(other, 0, 1), send_z(same, 2, 0), send_z(other, 2, 1)]
    *parts, left, right, packed[0] = tie(*parts, left, right, packed[0])
    blocks = [block, left, right]
    block = merge(info, parts)
    low, high, left, right, *packed = tie(
        send(left[:160], dx=1),
        send(right[160:], dx=-1),
        send(block, dx=1),
        send(block, dx=-1),
        *[send(part, dy=dy) if dy else part for dy, part in enumerate(packed)],
    )
    blocks += [low, high, block, left, right, send(left[:160], dx=1), send(right[160:], dx=-1)]
    new_master, new_first, new_second = update(info, packed, master, first_moment, second_moment)
    new_weights = place(info, blocks)
    return (new_master, new_first, new_second, new_weights)


def solution(mesh):
    in_specs = (
        P(("rep", "tp"), None),
        P("rep", "tp"),
        P(("rep", "tp"), None),
        P(("rep", "tp"), None),
        P(("rep", "tp"), None),
    )
    out_specs = (
        P(("rep", "tp"), None),
        P(("rep", "tp"), None),
        P(("rep", "tp"), None),
        P(None, "tp"),
    )
    return jax.shard_map(
        on_device, mesh=mesh, in_specs=in_specs, out_specs=out_specs, check_vma=False
    )
```

```python
import functools

import jax
import jax.numpy as jnp
import numpy as np
from jax import lax
from jax.experimental import pallas as pl
from jax.experimental.pallas import tpu as pltpu
from jax.sharding import PartitionSpec as P

STEP = 10

beta_one = 0.9
beta_two = 0.95
outer_rate = 0.05
weight_decay = 0.1
epsilon = 1e-08

BOTH = ("rep", "tp")
BF16, F32 = jnp.bfloat16, jnp.float32
MIB = 1024 * 1024
SMEM = pl.BlockSpec(memory_space=pltpu.SMEM)
VMEM = pl.BlockSpec(memory_space=pltpu.VMEM)
ANY = pl.BlockSpec(memory_space=pl.ANY)

ACROSS = (2, 1, 3, 0)
CHUNKS = (((0, 1), (0, 0)), ((2, 0), (2, 1)), ((1, 0), (1, 1)), ((3, 0), (3, 1)))
ALONE = ((0,), (1,), (2,), (3,))
CUTS = {2: ((0, 2), (1, 3)), 1: ALONE, 3: ALONE, 0: ALONE}
PIECES = tuple((dy, dh, dc) for dh in range(2) for dy in (0, 3, 1, 2) for dc in range(2))
PAIRS = ((1, 3), (0, 2))


def facts():
    rows = []
    for rep in range(16):
        for tp in range(16):
            x, zlo = rep // 4, rep % 4
            row = [x, zlo, tp // 4, tp // 2 % 2, tp % 2]
            row += [
                ((x + dx) % 4 * 4 + (zlo - j) % 4) * 160 for pair in PAIRS for dx in (0, 3, 1, 2) for j in pair
            ]
            y, zhi, core = row[2:5]
            row += [((y + dy) % 4 * 4 + (zhi ^ dh) * 2 + (core ^ dc)) * 128 for dy, dh, dc in PIECES]
            rows.append(row)
    return np.asarray(rows, np.int32)


X, ZLO, Y, ZHI, CORE, PLACE, TOKEN = 0, 1, 2, 3, 4, 5, 21


def pairs(move):
    def index(x, z, y, c):
        x, z, y, c = x % 4, z % 8, y % 4, c % 2
        return (x * 4 + z % 4) * 16 + y * 4 + (z // 4) * 2 + c

    return [
        (index(x, z, y, c), index(*move(x, z, y, c)))
        for x in range(4)
        for z in range(8)
        for y in range(4)
        for c in range(2)
    ]


def send(value, dx=0, dz=0, dy=0, dc=0):
    return lax.ppermute(value, BOTH, pairs(lambda x, z, y, c: (x + dx, z + dz, y + dy, c + dc)))


def send_z(value, j, h):
    def move(x, z, y, c):
        return x, (z // 4 ^ h) * 4 + (z + j) % 4, y, c

    return lax.ppermute(value, BOTH, pairs(move))


def call(kernel, name, out_shape, in_specs, out_specs, args, scratch=(), limit=16, size=1024):
    return pl.pallas_call(
        kernel,
        out_shape=out_shape,
        in_specs=in_specs,
        out_specs=out_specs,
        scratch_shapes=list(scratch),
        compiler_params=pltpu.CompilerParams(vmem_limit_bytes=limit * MIB),
        cost_estimate=pl.CostEstimate(flops=0, bytes_accessed=size, transcendentals=0),
        name=name,
    )(*args)


def prepare_kernel(info, rows, out, half_a, half_b, turned, ordered):
    for k in range(20):
        turned[k * 128 : (k + 1) * 128, :] = rows[:, k * 128 : (k + 1) * 128].astype(F32).T
    at = 0
    for dx in ACROSS:
        for j in range(4):
            start = lax.rem(info[X] + dx, 4) * 640 + lax.rem(info[ZLO] + j, 4) * 160
            for zhi in range(2):
                for y in range(4):
                    ordered[at : at + 20, :] = turned[pl.ds(start + y * 40 + zhi * 20, 20), :]
                    at += 20
    half_a[...] = ordered[:1280, :].astype(BF16)
    half_b[...] = ordered[1280:, :].astype(BF16)
    out[...] = ordered[...].astype(BF16)


def prepare(info, features):
    return call(
        prepare_kernel,
        "prepare",
        [jax.ShapeDtypeStruct((2560, 128), BF16)] + [jax.ShapeDtypeStruct((1280, 128), BF16)] * 2,
        [SMEM, VMEM],
        [VMEM] * 3,
        (info, features),
        [pltpu.VMEM((2560, 128), F32), pltpu.VMEM((2560, 128), F32)],
    )


def fetch_kernel(info, g, _, out):
    for k in range(16):
        start = pl.multiple_of(info[TOKEN + k], 128)
        out[k * 128 : (k + 1) * 128, :] = g[pl.ds(start, 128), :]


def fetch(info, g, after):
    return call(
        fetch_kernel,
        "fetch",
        jax.ShapeDtypeStruct((2048, 896), BF16),
        [SMEM, VMEM, ANY],
        VMEM,
        (info, g, after),
        size=4 * MIB,
    )


def term_kernel(firsts, cuts, info, *refs):
    pieces, g, outs, total = refs[:16], refs[16], refs[17:-1], refs[-1]
    rows = jnp.concatenate([piece[first : first + 640, :] for piece, first in zip(pieces, firsts)], axis=1)
    for start in range(0, 896, 256):
        stop = min(start + 256, 896)
        total[:, start:stop] = jnp.dot(rows, g[:, start:stop], preferred_element_type=F32)
    for out, cut in zip(outs, cuts):
        for k, (j, h) in enumerate(piece for chunk in cut for piece in CHUNKS[chunk]):
            at = pl.multiple_of(j * 160 + lax.rem(info[ZHI] + h, 2) * 80, 16)
            out[k * 80 : (k + 1) * 80, :] = total[pl.ds(at, 80), :].astype(BF16)


def term_rows(dx, info, pieces, g):
    arrays, firsts = zip(*pieces)
    return call(
        functools.partial(term_kernel, firsts, CUTS[dx]),
        "term_rows",
        [jax.ShapeDtypeStruct((160 * len(cut), 896), BF16) for cut in CUTS[dx]],
        [SMEM] + [VMEM] * 17,
        [VMEM] * len(CUTS[dx]),
        (info, *arrays, g),
        [pltpu.VMEM((640, 896), F32)],
        limit=24,
    )


def step(pseudo, old, first, second):
    moved = beta_one * first + (1.0 - beta_one) * pseudo
    spread = beta_two * second + (1.0 - beta_two) * pseudo * pseudo
    lead = (beta_one * moved + (1.0 - beta_one) * pseudo) / (1.0 - beta_one ** (STEP + 1))
    scale = spread / (1.0 - beta_two**STEP)
    value = old - outer_rate * (lead / (jnp.sqrt(scale) + epsilon) + weight_decay * old)
    return value, moved, spread


def columns(info, dy, flip, core):
    at = (lax.rem(info[Y] + 4 + dy, 4) * 4 + lax.rem(info[ZHI] + flip, 2) * 2 + core) * 896
    return (slice(None), pl.ds(pl.multiple_of(at, 128), 896))


def state_kernel(info, master, first, second, *refs):
    outs, rows = refs[:4], refs[4]
    for dy, out in enumerate(outs):
        for core in range(2):
            for flip in range(2):
                block = columns(info, dy, flip, core)
                old = master[block]
                top = old.astype(BF16).astype(F32)
                rows[0:10, :] = top
                rows[10:20, :] = old - top
                rows[20:30, :] = first[block]
                rows[30:40, :] = second[block]
                out[core, flip] = rows[...].astype(BF16)


def state(info, master, first, second):
    return call(
        state_kernel,
        "state",
        [jax.ShapeDtypeStruct((2, 2, 40, 896), BF16)] * 4,
        [SMEM] + [VMEM] * 3,
        [VMEM] * 4,
        (info, master, first, second),
        [pltpu.VMEM((40, 896), F32)],
    )


def state_core_kernel(info, *refs):
    parts, out = refs[:4], refs[4]
    for dy, part in enumerate(parts):
        out[lax.rem(info[Y] + 4 - dy, 4)] = part[1 - info[CORE]]


def state_core(info, parts):
    return call(
        state_core_kernel,
        "state_core",
        jax.ShapeDtypeStruct((4, 2, 40, 896), BF16),
        [SMEM] + [VMEM] * 4,
        VMEM,
        (info, *parts),
    )


def arrange_kernel(info, *refs):
    parts, other, out = refs[:4], refs[4], refs[5]
    core = info[CORE]
    for dy, part in enumerate(parts):
        at = lax.rem(info[Y] + 4 - dy, 4) * 2
        for flip in range(2):
            out[flip, at + core] = part[core, flip]
    for y in range(4):
        for flip in range(2):
            out[flip, 2 * y + 1 - core] = other[y, flip]


def arrange(info, parts, other):
    return call(
        arrange_kernel,
        "arrange",
        jax.ShapeDtypeStruct((2, 8, 40, 896), BF16),
        [SMEM] + [VMEM] * 5,
        VMEM,
        (info, *parts, other),
    )


def weights_kernel(info, *refs):
    parts, held, outs, mine, theirs, rows, groups = refs[:8], refs[8], refs[9:11], refs[11], refs[12], refs[13], refs[14]
    for h, out in enumerate(outs):
        block = [parts[4 * h + j][...].astype(F32) for j in range(4)]
        total = (block[0] + block[1]) + (block[2] + block[3])
        for k in range(8):
            gradient = total[k * 10 : (k + 1) * 10, :]
            groups[h, k] = gradient
            kept = held[h, k].astype(F32)
            value, _, _ = step(gradient / 16.0, kept[0:10, :] + kept[10:20, :], kept[20:30, :], kept[30:40, :])
            rows[k * 10 : (k + 1) * 10, :] = value
        out[...] = rows[...].astype(BF16)
    for y in range(4):
        for h in range(2):
            mine[y, h] = groups[h, 2 * y + info[CORE]].astype(BF16)
            theirs[y, h] = groups[h, 2 * y + 1 - info[CORE]].astype(BF16)


def weights(info, parts, held):
    return call(
        weights_kernel,
        "weights",
        [jax.ShapeDtypeStruct((80, 896), BF16)] * 2 + [jax.ShapeDtypeStruct((4, 2, 10, 896), BF16)] * 2,
        [SMEM] + [VMEM] * 9,
        [VMEM] * 4,
        (info, *parts, held),
        [pltpu.VMEM((80, 896), F32), pltpu.VMEM((2, 8, 10, 896), F32)],
    )


def pack_kernel(info, mine, other, *outs):
    for dy, out in enumerate(outs):
        y = lax.rem(info[Y] + dy, 4)
        out[0] = mine[y]
        out[1] = other[y]


def pack(info, mine, other):
    return call(
        pack_kernel,
        "pack",
        [jax.ShapeDtypeStruct((2, 2, 10, 896), BF16)] * 4,
        [SMEM] + [VMEM] * 2,
        [VMEM] * 4,
        (info, mine, other),
    )


def update_kernel(info, *refs):
    parts, (master, first, second) = refs[:4], refs[4:7]
    new_master, new_first, new_second = refs[7:]
    for dy, part in enumerate(parts):
        for dc in range(2):
            for flip in range(2):
                block = columns(info, -dy, flip, lax.rem(info[CORE] + dc, 2))
                value, moved, spread = step(
                    part[dc, flip].astype(F32) / 16.0, master[block], first[block], second[block]
                )
                new_master[block] = value
                new_first[block] = moved
                new_second[block] = spread


def update(info, parts, master, first, second):
    return call(
        update_kernel,
        "update",
        [jax.ShapeDtypeStruct((10, 14336), F32)] * 3,
        [SMEM] + [VMEM] * 7,
        [VMEM] * 3,
        (info, *parts, master, first, second),
    )


def merge_kernel(info, *refs):
    parts, out, rows = refs[:4], refs[4], refs[5]
    low = info[ZHI] == 0
    for n in range(2):
        mine, far = parts[2 * n][...].astype(F32), parts[2 * n + 1][...].astype(F32)
        for k, block in enumerate((jnp.where(low, mine, far), jnp.where(low, far, mine))):
            for y in range(4):
                at = n * 160 + y * 40 + k * 20
                rows[at : at + 20, :] = block[y * 20 : (y + 1) * 20, :]
    out[...] = rows[...].astype(BF16)


def merge(info, parts):
    return call(
        merge_kernel,
        "merge",
        jax.ShapeDtypeStruct((320, 896), BF16),
        [SMEM] + [VMEM] * 4,
        VMEM,
        (info, *parts),
        [pltpu.VMEM((320, 896), F32)],
    )


def place_kernel(info, *refs):
    blocks, out, sem = refs[:10], refs[10], refs[11]
    k = 0
    for block in blocks:
        for first in range(0, block.shape[0], 160):
            at = pl.multiple_of(info[PLACE + k], 32)
            pltpu.make_async_copy(
                block.at[pl.ds(first, 160), :], out.at[pl.ds(at, 160), :], sem
            ).start()
            k += 1
    pltpu.make_async_copy(out, out, sem).wait()


def place(info, blocks):
    return call(
        place_kernel,
        "place",
        jax.ShapeDtypeStruct((2560, 896), BF16),
        [SMEM] + [VMEM] * 10,
        ANY,
        (info, *blocks),
        [pltpu.SemaphoreType.DMA],
    )


def tie(*values):
    return lax.optimization_barrier(values)


def on_device(features, cotangent, master, first_moment, second_moment):
    device = lax.axis_index("rep") * 16 + lax.axis_index("tp")
    info = lax.dynamic_index_in_dim(jnp.asarray(facts()), device, 0, keepdims=False)

    own, half_a, half_b = prepare(info, features)
    held = list(state(info, master, first_moment, second_moment))
    a_here, left, right, own, half_b, held[1], held[3], g = tie(
        send(half_a, dz=4),
        send(own, dy=1),
        send(own, dy=-1),
        own,
        half_b,
        send(held[1], dy=1),
        send(held[3], dy=3),
        fetch(info, cotangent, own),
    )
    b_here, a_left, a_right = send(half_b, dz=4), send(a_here, dy=1), send(a_here, dy=-1)
    opposite_a, opposite_b = send(left[:1280], dy=1), send(right[1280:], dy=-1)
    opposite_a, opposite_b, left, right, a_here, own_c = tie(
        opposite_a, opposite_b, left, right, a_here, send(own, dc=1)
    )
    left_c, right_c, a_here_c = send(left, dc=1), send(right, dc=1), send(a_here, dc=1)
    b_here, a_left, a_right, left_c, right_c, a_here_c, opposite_a, opposite_b = tie(
        b_here, a_left, a_right, left_c, right_c, a_here_c, opposite_a, opposite_b
    )
    a_two, a_one = send(a_left[:640], dy=1), send(a_right[640:], dy=-1)
    b_left, b_right, b_here_c = send(b_here, dy=1), send(b_here, dy=-1), send(b_here, dc=1)
    a_two, a_one, a_left, a_right, opposite_a, opposite_b, b_here_c = tie(
        a_two, a_one, a_left, a_right, opposite_a, opposite_b, b_here_c
    )
    a_two_c, a_one_c = send(a_two, dc=1), send(a_one, dc=1)
    a_left_c, a_right_c = send(a_left, dc=1), send(a_right, dc=1)
    opposite_a_c, opposite_b_c = send(opposite_a, dc=1), send(opposite_b, dc=1)
    a_two_c, a_one_c, a_left_c, a_right_c, opposite_a_c, opposite_b_c, b_left, b_right = tie(
        a_two_c, a_one_c, a_left_c, a_right_c, opposite_a_c, opposite_b_c, b_left, b_right
    )
    b_three, b_none = send(b_left[:640], dy=1), send(b_right[640:], dy=-1)

    def around(dx, *more):
        first = 640 * ACROSS.index(dx)
        pieces = [own, own_c, left, left_c, right, right_c]
        if first < 1280:
            pieces += [opposite_a, opposite_a_c, a_here, a_here_c, a_left, a_left_c, a_right, a_right_c]
        else:
            pieces += [opposite_b, opposite_b_c, b_here, b_here_c, b_left, b_left_c, b_right, b_right_c]
        return [(piece, first % piece.shape[0]) for piece in pieces + list(more)]

    def add(first, *others):
        total = first.astype(F32)
        for other in others:
            total = total + other.astype(F32)
        return total.astype(BF16)

    def cut(total, chunk):
        result = {}
        for i, (j, h) in enumerate(CHUNKS[chunk]):
            part = total[i * 80 : (i + 1) * 80]
            result[j, h] = part if (j, h) == (0, 0) else send_z(part, j, h)
        return result

    two_ac, two_bd = term_rows(2, info, around(2, a_two, a_two_c), g)
    two_ac, two_bd = tie(send(two_ac, dx=1), send(two_bd, dx=-1))
    ahead = term_rows(1, info, around(1, a_one, a_one_c), g)
    b_left, b_right, b_three, b_none, *ahead = tie(b_left, b_right, b_three, b_none, *ahead)
    plain_b = send(ahead[1], dx=1)
    b_left_c, b_right_c = send(b_left, dc=1), send(b_right, dc=1)
    b_three_c, b_none_c = send(b_three, dc=1), send(b_none, dc=1)
    carried_a = add(ahead[0], two_ac[:160])
    behind = term_rows(3, info, around(3, b_three, b_three_c), g)
    plain_a = send(behind[0], dx=-1)
    carried_b = add(behind[1], two_bd[:160])
    carried_a, carried_b = send(carried_a, dx=1), send(carried_b, dx=-1)
    plain_d, plain_c, _, _ = tie(ahead[3], behind[2], two_ac, two_bd)
    plain_d, plain_c = send(plain_d, dx=1), send(plain_c, dx=-1)
    here = term_rows(0, info, around(0, b_none, b_none_c), g)
    carried_c, carried_d = add(ahead[2], two_ac[160:]), add(behind[3], two_bd[160:])
    sum_a, sum_b = add(here[0], plain_a, carried_a), add(here[1], plain_b, carried_b)
    carried_c, carried_d, sum_a, sum_b, held[2] = tie(carried_c, carried_d, sum_a, sum_b, held[2])
    held[2] = send(held[2], dy=2)
    carried_c, carried_d = send(carried_c, dx=1), send(carried_d, dx=-1)
    parts = {**cut(sum_a, 0), **cut(sum_b, 1)}
    plain_c, plain_d, carried_c, carried_d, held[2] = tie(plain_c, plain_d, carried_c, carried_d, held[2])
    parts.update(cut(add(here[2], plain_c, carried_c), 2))
    parts.update(cut(add(here[3], plain_d, carried_d), 3))
    held = arrange(info, held, send(state_core(info, held), dc=1))
    same, other, mine, theirs = weights(info, [parts[j, h] for h in range(2) for j in range(4)], held)

    packed = list(pack(info, mine, send(theirs, dc=1)))
    parts = [send_z(value, j, h) for j in PAIRS[0] for h, value in enumerate((same, other))]
    *parts, same, other, packed[1] = tie(*parts, same, other, send(packed[1], dy=1))
    block = merge(info, parts)
    parts = [same, send_z(other, 0, 1), send_z(same, 2, 0), send_z(other, 2, 1)]
    *parts, left, right, packed[2] = tie(
        *parts, send(block, dx=1), send(block, dx=-1), send(packed[2], dy=2)
    )
    blocks = [block, left, right]
    block = merge(info, parts)
    low, high, left, right, packed[3] = tie(
        send(left[:160], dx=1),
        send(right[160:], dx=-1),
        send(block, dx=1),
        send(block, dx=-1),
        send(packed[3], dy=3),
    )
    blocks += [low, high, block, left, right, send(left[:160], dx=1), send(right[160:], dx=-1)]
    new_master, new_first, new_second = update(info, packed, master, first_moment, second_moment)
    new_weights = place(info, blocks)
    return (new_master, new_first, new_second, new_weights)


def solution(mesh):
    in_specs = (
        P(("rep", "tp"), None),
        P("rep", "tp"),
        P(("rep", "tp"), None),
        P(("rep", "tp"), None),
        P(("rep", "tp"), None),
    )
    out_specs = (
        P(("rep", "tp"), None),
        P(("rep", "tp"), None),
        P(("rep", "tp"), None),
        P(None, "tp"),
    )
    return jax.shard_map(
        on_device, mesh=mesh, in_specs=in_specs, out_specs=out_specs, check_vma=False
    )
```

```python
import functools

import jax
import jax.numpy as jnp
import numpy as np
from jax import lax
from jax.experimental import pallas as pl
from jax.experimental.pallas import tpu as pltpu
from jax.sharding import PartitionSpec as P

STEP = 10

beta_one = 0.9
beta_two = 0.95
outer_rate = 0.05
weight_decay = 0.1
epsilon = 1e-08

BOTH = ("rep", "tp")
BF16, F32 = jnp.bfloat16, jnp.float32
MIB = 1024 * 1024
SMEM = pl.BlockSpec(memory_space=pltpu.SMEM)
VMEM = pl.BlockSpec(memory_space=pltpu.VMEM)
ANY = pl.BlockSpec(memory_space=pl.ANY)

ACROSS = (2, 1, 3, 0)
CHUNKS = (((0, 1), (0, 0)), ((2, 0), (2, 1)), ((1, 0), (1, 1)), ((3, 0), (3, 1)))
ALONE = ((0,), (1,), (2,), (3,))
CUTS = {2: ((0, 2), (1, 3)), 1: ALONE, 3: ALONE, 0: ALONE}
PIECES = tuple((dy, dh, dc) for dh in range(2) for dy in (0, 3, 1, 2) for dc in range(2))
PAIRS = ((1, 3), (0, 2))


def facts():
    rows = []
    for rep in range(16):
        for tp in range(16):
            x, zlo = rep // 4, rep % 4
            row = [x, zlo, tp // 4, tp // 2 % 2, tp % 2]
            row += [
                ((x + dx) % 4 * 4 + (zlo - j) % 4) * 160 for pair in PAIRS for dx in (0, 3, 1, 2) for j in pair
            ]
            y, zhi, core = row[2:5]
            row += [((y + dy) % 4 * 4 + (zhi ^ dh) * 2 + (core ^ dc)) * 128 for dy, dh, dc in PIECES]
            rows.append(row)
    return np.asarray(rows, np.int32)


X, ZLO, Y, ZHI, CORE, PLACE, TOKEN = 0, 1, 2, 3, 4, 5, 21


def pairs(move):
    def index(x, z, y, c):
        x, z, y, c = x % 4, z % 8, y % 4, c % 2
        return (x * 4 + z % 4) * 16 + y * 4 + (z // 4) * 2 + c

    return [
        (index(x, z, y, c), index(*move(x, z, y, c)))
        for x in range(4)
        for z in range(8)
        for y in range(4)
        for c in range(2)
    ]


def send(value, dx=0, dz=0, dy=0, dc=0):
    return lax.ppermute(value, BOTH, pairs(lambda x, z, y, c: (x + dx, z + dz, y + dy, c + dc)))


def send_z(value, j, h):
    def move(x, z, y, c):
        return x, (z // 4 ^ h) * 4 + (z + j) % 4, y, c

    return lax.ppermute(value, BOTH, pairs(move))


def call(kernel, name, out_shape, in_specs, out_specs, args, scratch=(), limit=16, size=1024):
    return pl.pallas_call(
        kernel,
        out_shape=out_shape,
        in_specs=in_specs,
        out_specs=out_specs,
        scratch_shapes=list(scratch),
        compiler_params=pltpu.CompilerParams(vmem_limit_bytes=limit * MIB),
        cost_estimate=pl.CostEstimate(flops=0, bytes_accessed=size, transcendentals=0),
        name=name,
    )(*args)


def prepare_kernel(info, rows, out, half_a, half_b, turned, ordered):
    for k in range(20):
        turned[k * 128 : (k + 1) * 128, :] = rows[:, k * 128 : (k + 1) * 128].astype(F32).T
    at = 0
    for dx in ACROSS:
        for j in range(4):
            start = lax.rem(info[X] + dx, 4) * 640 + lax.rem(info[ZLO] + j, 4) * 160
            for zhi in range(2):
                for y in range(4):
                    ordered[at : at + 20, :] = turned[pl.ds(start + y * 40 + zhi * 20, 20), :]
                    at += 20
    half_a[...] = ordered[:1280, :].astype(BF16)
    half_b[...] = ordered[1280:, :].astype(BF16)
    out[...] = ordered[...].astype(BF16)


def prepare(info, features):
    return call(
        prepare_kernel,
        "prepare",
        [jax.ShapeDtypeStruct((2560, 128), BF16)] + [jax.ShapeDtypeStruct((1280, 128), BF16)] * 2,
        [SMEM, VMEM],
        [VMEM] * 3,
        (info, features),
        [pltpu.VMEM((2560, 128), F32), pltpu.VMEM((2560, 128), F32)],
    )


def fetch_kernel(info, g, _, out):
    for k in range(16):
        start = pl.multiple_of(info[TOKEN + k], 128)
        out[k * 128 : (k + 1) * 128, :] = g[pl.ds(start, 128), :]


def fetch(info, g, after):
    return call(
        fetch_kernel,
        "fetch",
        jax.ShapeDtypeStruct((2048, 896), BF16),
        [SMEM, VMEM, ANY],
        VMEM,
        (info, g, after),
        size=4 * MIB,
    )


def term_kernel(firsts, cuts, info, *refs):
    pieces, g, outs, total = refs[:16], refs[16], refs[17:-1], refs[-1]
    rows = jnp.concatenate([piece[first : first + 640, :] for piece, first in zip(pieces, firsts)], axis=1)
    for start in range(0, 896, 256):
        stop = min(start + 256, 896)
        total[:, start:stop] = jnp.dot(rows, g[:, start:stop], preferred_element_type=F32)
    for out, cut in zip(outs, cuts):
        for k, (j, h) in enumerate(piece for chunk in cut for piece in CHUNKS[chunk]):
            at = pl.multiple_of(j * 160 + lax.rem(info[ZHI] + h, 2) * 80, 16)
            out[k * 80 : (k + 1) * 80, :] = total[pl.ds(at, 80), :].astype(BF16)


def term_rows(dx, info, pieces, g):
    arrays, firsts = zip(*pieces)
    return call(
        functools.partial(term_kernel, firsts, CUTS[dx]),
        "term_rows",
        [jax.ShapeDtypeStruct((160 * len(cut), 896), BF16) for cut in CUTS[dx]],
        [SMEM] + [VMEM] * 17,
        [VMEM] * len(CUTS[dx]),
        (info, *arrays, g),
        [pltpu.VMEM((640, 896), F32)],
        limit=24,
    )


def step(pseudo, old, first, second):
    moved = beta_one * first + (1.0 - beta_one) * pseudo
    spread = beta_two * second + (1.0 - beta_two) * pseudo * pseudo
    lead = (beta_one * moved + (1.0 - beta_one) * pseudo) / (1.0 - beta_one ** (STEP + 1))
    scale = spread / (1.0 - beta_two**STEP)
    value = old - outer_rate * (lead / (jnp.sqrt(scale) + epsilon) + weight_decay * old)
    return value, moved, spread


def columns(info, dy, flip, core):
    at = (lax.rem(info[Y] + 4 + dy, 4) * 4 + lax.rem(info[ZHI] + flip, 2) * 2 + core) * 896
    return (slice(None), pl.ds(pl.multiple_of(at, 128), 896))


def state_kernel(info, master, first, second, *refs):
    outs, rows = refs[:4], refs[4]
    for dy, out in enumerate(outs):
        for core in range(2):
            for flip in range(2):
                block = columns(info, dy, flip, core)
                old = master[block]
                top = old.astype(BF16).astype(F32)
                rows[0:10, :] = top
                rows[10:20, :] = old - top
                rows[20:30, :] = first[block]
                rows[30:40, :] = second[block]
                out[core, flip] = rows[...].astype(BF16)


def state(info, master, first, second):
    return call(
        state_kernel,
        "state",
        [jax.ShapeDtypeStruct((2, 2, 40, 896), BF16)] * 4,
        [SMEM] + [VMEM] * 3,
        [VMEM] * 4,
        (info, master, first, second),
        [pltpu.VMEM((40, 896), F32)],
    )


def state_core_kernel(info, *refs):
    parts, out = refs[:4], refs[4]
    for dy, part in enumerate(parts):
        out[lax.rem(info[Y] + 4 - dy, 4)] = part[1 - info[CORE]]


def state_core(info, parts):
    return call(
        state_core_kernel,
        "state_core",
        jax.ShapeDtypeStruct((4, 2, 40, 896), BF16),
        [SMEM] + [VMEM] * 4,
        VMEM,
        (info, *parts),
    )


def arrange_kernel(info, *refs):
    parts, other, out = refs[:4], refs[4], refs[5]
    core = info[CORE]
    for dy, part in enumerate(parts):
        at = lax.rem(info[Y] + 4 - dy, 4) * 2
        for flip in range(2):
            out[flip, at + core] = part[core, flip]
    for y in range(4):
        for flip in range(2):
            out[flip, 2 * y + 1 - core] = other[y, flip]


def arrange(info, parts, other):
    return call(
        arrange_kernel,
        "arrange",
        jax.ShapeDtypeStruct((2, 8, 40, 896), BF16),
        [SMEM] + [VMEM] * 5,
        VMEM,
        (info, *parts, other),
    )


def weights_kernel(info, *refs):
    parts, held, outs, mine, theirs, rows, groups = refs[:8], refs[8], refs[9:11], refs[11], refs[12], refs[13], refs[14]
    for h, out in enumerate(outs):
        block = [parts[4 * h + j][...].astype(F32) for j in range(4)]
        total = (block[0] + block[1]) + (block[2] + block[3])
        for k in range(8):
            gradient = total[k * 10 : (k + 1) * 10, :]
            groups[h, k] = gradient
            kept = held[h, k].astype(F32)
            value, _, _ = step(gradient / 16.0, kept[0:10, :] + kept[10:20, :], kept[20:30, :], kept[30:40, :])
            rows[k * 10 : (k + 1) * 10, :] = value
        out[...] = rows[...].astype(BF16)
    for y in range(4):
        for h in range(2):
            mine[y, h] = groups[h, 2 * y + info[CORE]].astype(BF16)
            theirs[y, h] = groups[h, 2 * y + 1 - info[CORE]].astype(BF16)


def weights(info, parts, held):
    return call(
        weights_kernel,
        "weights",
        [jax.ShapeDtypeStruct((80, 896), BF16)] * 2 + [jax.ShapeDtypeStruct((4, 2, 10, 896), BF16)] * 2,
        [SMEM] + [VMEM] * 9,
        [VMEM] * 4,
        (info, *parts, held),
        [pltpu.VMEM((80, 896), F32), pltpu.VMEM((2, 8, 10, 896), F32)],
    )


def pack_kernel(info, mine, other, *outs):
    for dy, out in enumerate(outs):
        y = lax.rem(info[Y] + dy, 4)
        out[0] = mine[y]
        out[1] = other[y]


def pack(info, mine, other):
    return call(
        pack_kernel,
        "pack",
        [jax.ShapeDtypeStruct((2, 2, 10, 896), BF16)] * 4,
        [SMEM] + [VMEM] * 2,
        [VMEM] * 4,
        (info, mine, other),
    )


def update_kernel(info, *refs):
    parts, (master, first, second) = refs[:4], refs[4:7]
    new_master, new_first, new_second = refs[7:]
    for dy, part in enumerate(parts):
        for dc in range(2):
            for flip in range(2):
                block = columns(info, -dy, flip, lax.rem(info[CORE] + dc, 2))
                value, moved, spread = step(
                    part[dc, flip].astype(F32) / 16.0, master[block], first[block], second[block]
                )
                new_master[block] = value
                new_first[block] = moved
                new_second[block] = spread


def update(info, parts, master, first, second):
    return call(
        update_kernel,
        "update",
        [jax.ShapeDtypeStruct((10, 14336), F32)] * 3,
        [SMEM] + [VMEM] * 7,
        [VMEM] * 3,
        (info, *parts, master, first, second),
    )


def merge_kernel(info, *refs):
    parts, out, rows = refs[:4], refs[4], refs[5]
    low = info[ZHI] == 0
    for n in range(2):
        mine, far = parts[2 * n][...].astype(F32), parts[2 * n + 1][...].astype(F32)
        for k, block in enumerate((jnp.where(low, mine, far), jnp.where(low, far, mine))):
            for y in range(4):
                at = n * 160 + y * 40 + k * 20
                rows[at : at + 20, :] = block[y * 20 : (y + 1) * 20, :]
    out[...] = rows[...].astype(BF16)


def merge(info, parts):
    return call(
        merge_kernel,
        "merge",
        jax.ShapeDtypeStruct((320, 896), BF16),
        [SMEM] + [VMEM] * 4,
        VMEM,
        (info, *parts),
        [pltpu.VMEM((320, 896), F32)],
    )


def place_kernel(info, *refs):
    blocks, out, sem = refs[:10], refs[10], refs[11]
    k = 0
    for block in blocks:
        for first in range(0, block.shape[0], 160):
            at = pl.multiple_of(info[PLACE + k], 32)
            pltpu.make_async_copy(
                block.at[pl.ds(first, 160), :], out.at[pl.ds(at, 160), :], sem
            ).start()
            k += 1
    pltpu.make_async_copy(out, out, sem).wait()


def place(info, blocks):
    return call(
        place_kernel,
        "place",
        jax.ShapeDtypeStruct((2560, 896), BF16),
        [SMEM] + [VMEM] * 10,
        ANY,
        (info, *blocks),
        [pltpu.SemaphoreType.DMA],
    )


def tie(*values):
    return lax.optimization_barrier(values)


def on_device(features, cotangent, master, first_moment, second_moment):
    device = lax.axis_index("rep") * 16 + lax.axis_index("tp")
    info = lax.dynamic_index_in_dim(jnp.asarray(facts()), device, 0, keepdims=False)

    own, half_a, half_b = prepare(info, features)
    held = list(state(info, master, first_moment, second_moment))
    a_here, left, right, own, half_b, held[1], held[3], g = tie(
        send(half_a, dz=4),
        send(own, dy=1),
        send(own, dy=-1),
        own,
        half_b,
        send(held[1], dy=1),
        send(held[3], dy=3),
        fetch(info, cotangent, own),
    )
    b_here, a_left, a_right = send(half_b, dz=4), send(a_here, dy=1), send(a_here, dy=-1)
    opposite_a, opposite_b = send(left[:1280], dy=1), send(right[1280:], dy=-1)
    opposite_a, opposite_b, left, right, a_here, own_c = tie(
        opposite_a, opposite_b, left, right, a_here, send(own, dc=1)
    )
    left_c, right_c, a_here_c = send(left, dc=1), send(right, dc=1), send(a_here, dc=1)
    b_here, a_left, a_right, left_c, right_c, a_here_c, opposite_a, opposite_b = tie(
        b_here, a_left, a_right, left_c, right_c, a_here_c, opposite_a, opposite_b
    )
    a_two, a_one = send(a_left[:640], dy=1), send(a_right[640:], dy=-1)
    b_here_c = send(b_here, dc=1)
    a_two, a_one, a_left, a_right, opposite_a, opposite_b, b_here, b_here_c = tie(
        a_two, a_one, a_left, a_right, opposite_a, opposite_b, b_here, b_here_c
    )
    b_left, b_right = send(b_here, dy=1), send(b_here, dy=-1)
    a_two_c, a_one_c = send(a_two, dc=1), send(a_one, dc=1)
    a_left_c, a_right_c = send(a_left, dc=1), send(a_right, dc=1)
    opposite_a_c, opposite_b_c = send(opposite_a, dc=1), send(opposite_b, dc=1)
    a_two_c, a_one_c, a_left_c, a_right_c, opposite_a_c, opposite_b_c = tie(
        a_two_c, a_one_c, a_left_c, a_right_c, opposite_a_c, opposite_b_c
    )

    def around(dx, *more):
        first = 640 * ACROSS.index(dx)
        pieces = [own, own_c, left, left_c, right, right_c]
        if first < 1280:
            pieces += [opposite_a, opposite_a_c, a_here, a_here_c, a_left, a_left_c, a_right, a_right_c]
        else:
            pieces += [opposite_b, opposite_b_c, b_here, b_here_c, b_left, b_left_c, b_right, b_right_c]
        return [(piece, first % piece.shape[0]) for piece in pieces + list(more)]

    def add(first, *others):
        total = first.astype(F32)
        for other in others:
            total = total + other.astype(F32)
        return total.astype(BF16)

    def cut(total, chunk):
        result = {}
        for i, (j, h) in enumerate(CHUNKS[chunk]):
            part = total[i * 80 : (i + 1) * 80]
            result[j, h] = part if (j, h) == (0, 0) else send_z(part, j, h)
        return result

    two_ac, two_bd = term_rows(2, info, around(2, a_two, a_two_c), g)
    two_ac, two_bd = tie(send(two_ac, dx=1), send(two_bd, dx=-1))
    b_three, b_none = send(b_left[:640], dy=1), send(b_right[640:], dy=-1)
    ahead = term_rows(1, info, around(1, a_one, a_one_c), g)
    b_left, b_right, b_three, b_none, *ahead = tie(b_left, b_right, b_three, b_none, *ahead)
    plain_b = send(ahead[1], dx=1)
    b_left_c, b_right_c = send(b_left, dc=1), send(b_right, dc=1)
    b_three_c, b_none_c = send(b_three, dc=1), send(b_none, dc=1)
    carried_a = add(ahead[0], two_ac[:160])
    behind = term_rows(3, info, around(3, b_three, b_three_c), g)
    plain_a = send(behind[0], dx=-1)
    carried_b = add(behind[1], two_bd[:160])
    carried_a, carried_b = send(carried_a, dx=1), send(carried_b, dx=-1)
    plain_d, plain_c, _, _ = tie(ahead[3], behind[2], two_ac, two_bd)
    plain_d, plain_c = send(plain_d, dx=1), send(plain_c, dx=-1)
    here = term_rows(0, info, around(0, b_none, b_none_c), g)
    carried_c, carried_d = add(ahead[2], two_ac[160:]), add(behind[3], two_bd[160:])
    sum_a, sum_b = add(here[0], plain_a, carried_a), add(here[1], plain_b, carried_b)
    carried_c, carried_d, sum_a, sum_b, held[2] = tie(carried_c, carried_d, sum_a, sum_b, held[2])
    held[2] = send(held[2], dy=2)
    carried_c, carried_d = send(carried_c, dx=1), send(carried_d, dx=-1)
    parts = {**cut(sum_a, 0), **cut(sum_b, 1)}
    plain_c, plain_d, carried_c, carried_d, held[2] = tie(plain_c, plain_d, carried_c, carried_d, held[2])
    parts.update(cut(add(here[2], plain_c, carried_c), 2))
    parts.update(cut(add(here[3], plain_d, carried_d), 3))
    held = arrange(info, held, send(state_core(info, held), dc=1))
    same, other, mine, theirs = weights(info, [parts[j, h] for h in range(2) for j in range(4)], held)

    packed = list(pack(info, mine, send(theirs, dc=1)))
    parts = [send_z(value, j, h) for j in PAIRS[0] for h, value in enumerate((same, other))]
    *parts, same, other, packed[1] = tie(*parts, same, other, send(packed[1], dy=1))
    block = merge(info, parts)
    parts = [same, send_z(other, 0, 1), send_z(same, 2, 0), send_z(other, 2, 1)]
    *parts, left, right, packed[2] = tie(*parts, send(block, dx=1), send(block, dx=-1), packed[2])
    blocks = [block, left, right]
    block = merge(info, parts)
    low, high, left, right, packed[2], packed[3] = tie(
        send(left[:160], dx=1),
        send(right[160:], dx=-1),
        send(block, dx=1),
        send(block, dx=-1),
        send(packed[2], dy=2),
        send(packed[3], dy=3),
    )
    blocks += [low, high, block, left, right, send(left[:160], dx=1), send(right[160:], dx=-1)]
    new_master, new_first, new_second = update(info, packed, master, first_moment, second_moment)
    new_weights = place(info, blocks)
    return (new_master, new_first, new_second, new_weights)


def solution(mesh):
    in_specs = (
        P(("rep", "tp"), None),
        P("rep", "tp"),
        P(("rep", "tp"), None),
        P(("rep", "tp"), None),
        P(("rep", "tp"), None),
    )
    out_specs = (
        P(("rep", "tp"), None),
        P(("rep", "tp"), None),
        P(("rep", "tp"), None),
        P(None, "tp"),
    )
    return jax.shard_map(
        on_device, mesh=mesh, in_specs=in_specs, out_specs=out_specs, check_vma=False
    )
```

```python
import functools

import jax
import jax.numpy as jnp
import numpy as np
from jax import lax
from jax.experimental import pallas as pl
from jax.experimental.pallas import tpu as pltpu
from jax.sharding import PartitionSpec as P

STEP = 10

beta_one = 0.9
beta_two = 0.95
outer_rate = 0.05
weight_decay = 0.1
epsilon = 1e-08

BOTH = ("rep", "tp")
BF16, F32 = jnp.bfloat16, jnp.float32
MIB = 1024 * 1024
SMEM = pl.BlockSpec(memory_space=pltpu.SMEM)
VMEM = pl.BlockSpec(memory_space=pltpu.VMEM)
ANY = pl.BlockSpec(memory_space=pl.ANY)

ACROSS = (2, 1, 3, 0)
CHUNKS = (((0, 1), (0, 0)), ((2, 0), (2, 1)), ((1, 0), (1, 1)), ((3, 0), (3, 1)))
ALONE = ((0,), (1,), (2,), (3,))
CUTS = {2: ((0, 2), (1, 3)), 1: ALONE, 3: ALONE, 0: ALONE}
PIECES = tuple((dy, dh, dc) for dh in range(2) for dy in (0, 3, 1, 2) for dc in range(2))
PAIRS = ((1, 3), (0, 2))


def facts():
    rows = []
    for rep in range(16):
        for tp in range(16):
            x, zlo = rep // 4, rep % 4
            row = [x, zlo, tp // 4, tp // 2 % 2, tp % 2]
            row += [
                ((x + dx) % 4 * 4 + (zlo - j) % 4) * 160 for pair in PAIRS for dx in (0, 3, 1, 2) for j in pair
            ]
            y, zhi, core = row[2:5]
            row += [((y + dy) % 4 * 4 + (zhi ^ dh) * 2 + (core ^ dc)) * 128 for dy, dh, dc in PIECES]
            rows.append(row)
    return np.asarray(rows, np.int32)


X, ZLO, Y, ZHI, CORE, PLACE, TOKEN = 0, 1, 2, 3, 4, 5, 21


def pairs(move):
    def index(x, z, y, c):
        x, z, y, c = x % 4, z % 8, y % 4, c % 2
        return (x * 4 + z % 4) * 16 + y * 4 + (z // 4) * 2 + c

    return [
        (index(x, z, y, c), index(*move(x, z, y, c)))
        for x in range(4)
        for z in range(8)
        for y in range(4)
        for c in range(2)
    ]


def send(value, dx=0, dz=0, dy=0, dc=0):
    return lax.ppermute(value, BOTH, pairs(lambda x, z, y, c: (x + dx, z + dz, y + dy, c + dc)))


def send_z(value, j, h):
    def move(x, z, y, c):
        return x, (z // 4 ^ h) * 4 + (z + j) % 4, y, c

    return lax.ppermute(value, BOTH, pairs(move))


def call(kernel, name, out_shape, in_specs, out_specs, args, scratch=(), limit=16, size=1024):
    return pl.pallas_call(
        kernel,
        out_shape=out_shape,
        in_specs=in_specs,
        out_specs=out_specs,
        scratch_shapes=list(scratch),
        compiler_params=pltpu.CompilerParams(vmem_limit_bytes=limit * MIB),
        cost_estimate=pl.CostEstimate(flops=0, bytes_accessed=size, transcendentals=0),
        name=name,
    )(*args)


def prepare_kernel(info, rows, out, half_a, half_b, turned, ordered):
    for k in range(20):
        turned[k * 128 : (k + 1) * 128, :] = rows[:, k * 128 : (k + 1) * 128].astype(F32).T
    at = 0
    for dx in ACROSS:
        for j in range(4):
            start = lax.rem(info[X] + dx, 4) * 640 + lax.rem(info[ZLO] + j, 4) * 160
            for zhi in range(2):
                for y in range(4):
                    ordered[at : at + 20, :] = turned[pl.ds(start + y * 40 + zhi * 20, 20), :]
                    at += 20
    half_a[...] = ordered[:1280, :].astype(BF16)
    half_b[...] = ordered[1280:, :].astype(BF16)
    out[...] = ordered[...].astype(BF16)


def prepare(info, features):
    return call(
        prepare_kernel,
        "prepare",
        [jax.ShapeDtypeStruct((2560, 128), BF16)] + [jax.ShapeDtypeStruct((1280, 128), BF16)] * 2,
        [SMEM, VMEM],
        [VMEM] * 3,
        (info, features),
        [pltpu.VMEM((2560, 128), F32), pltpu.VMEM((2560, 128), F32)],
    )


def fetch_kernel(info, g, _, out):
    for k in range(16):
        start = pl.multiple_of(info[TOKEN + k], 128)
        out[k * 128 : (k + 1) * 128, :] = g[pl.ds(start, 128), :]


def fetch(info, g, after):
    return call(
        fetch_kernel,
        "fetch",
        jax.ShapeDtypeStruct((2048, 896), BF16),
        [SMEM, VMEM, ANY],
        VMEM,
        (info, g, after),
        size=4 * MIB,
    )


def term_kernel(firsts, cuts, info, *refs):
    pieces, g, outs, total = refs[:16], refs[16], refs[17:-1], refs[-1]
    rows = jnp.concatenate([piece[first : first + 640, :] for piece, first in zip(pieces, firsts)], axis=1)
    for start in range(0, 896, 256):
        stop = min(start + 256, 896)
        total[:, start:stop] = jnp.dot(rows, g[:, start:stop], preferred_element_type=F32)
    for out, cut in zip(outs, cuts):
        for k, (j, h) in enumerate(piece for chunk in cut for piece in CHUNKS[chunk]):
            at = pl.multiple_of(j * 160 + lax.rem(info[ZHI] + h, 2) * 80, 16)
            out[k * 80 : (k + 1) * 80, :] = total[pl.ds(at, 80), :].astype(BF16)


def term_rows(dx, info, pieces, g):
    arrays, firsts = zip(*pieces)
    return call(
        functools.partial(term_kernel, firsts, CUTS[dx]),
        "term_rows",
        [jax.ShapeDtypeStruct((160 * len(cut), 896), BF16) for cut in CUTS[dx]],
        [SMEM] + [VMEM] * 17,
        [VMEM] * len(CUTS[dx]),
        (info, *arrays, g),
        [pltpu.VMEM((640, 896), F32)],
        limit=24,
    )


def step(pseudo, old, first, second):
    moved = beta_one * first + (1.0 - beta_one) * pseudo
    spread = beta_two * second + (1.0 - beta_two) * pseudo * pseudo
    lead = (beta_one * moved + (1.0 - beta_one) * pseudo) / (1.0 - beta_one ** (STEP + 1))
    scale = spread / (1.0 - beta_two**STEP)
    value = old - outer_rate * (lead / (jnp.sqrt(scale) + epsilon) + weight_decay * old)
    return value, moved, spread


def columns(info, dy, flip, core):
    at = (lax.rem(info[Y] + 4 + dy, 4) * 4 + lax.rem(info[ZHI] + flip, 2) * 2 + core) * 896
    return (slice(None), pl.ds(pl.multiple_of(at, 128), 896))


def state_kernel(info, master, first, second, *refs):
    outs, rows = refs[:4], refs[4]
    for dy, out in enumerate(outs):
        for core in range(2):
            for flip in range(2):
                block = columns(info, dy, flip, core)
                old = master[block]
                top = old.astype(BF16).astype(F32)
                rows[0:10, :] = top
                rows[10:20, :] = old - top
                rows[20:30, :] = first[block]
                rows[30:40, :] = second[block]
                out[core, flip] = rows[...].astype(BF16)


def state(info, master, first, second):
    return call(
        state_kernel,
        "state",
        [jax.ShapeDtypeStruct((2, 2, 40, 896), BF16)] * 4,
        [SMEM] + [VMEM] * 3,
        [VMEM] * 4,
        (info, master, first, second),
        [pltpu.VMEM((40, 896), F32)],
    )


def state_core_kernel(info, *refs):
    parts, out = refs[:4], refs[4]
    for dy, part in enumerate(parts):
        out[lax.rem(info[Y] + 4 - dy, 4)] = part[1 - info[CORE]]


def state_core(info, parts):
    return call(
        state_core_kernel,
        "state_core",
        jax.ShapeDtypeStruct((4, 2, 40, 896), BF16),
        [SMEM] + [VMEM] * 4,
        VMEM,
        (info, *parts),
    )


def arrange_kernel(info, *refs):
    parts, other, out = refs[:4], refs[4], refs[5]
    core = info[CORE]
    for dy, part in enumerate(parts):
        at = lax.rem(info[Y] + 4 - dy, 4) * 2
        for flip in range(2):
            out[flip, at + core] = part[core, flip]
    for y in range(4):
        for flip in range(2):
            out[flip, 2 * y + 1 - core] = other[y, flip]


def arrange(info, parts, other):
    return call(
        arrange_kernel,
        "arrange",
        jax.ShapeDtypeStruct((2, 8, 40, 896), BF16),
        [SMEM] + [VMEM] * 5,
        VMEM,
        (info, *parts, other),
    )


def weights_kernel(info, *refs):
    parts, held, outs, mine, theirs, rows, groups = refs[:8], refs[8], refs[9:11], refs[11], refs[12], refs[13], refs[14]
    for h, out in enumerate(outs):
        block = [parts[4 * h + j][...].astype(F32) for j in range(4)]
        total = (block[0] + block[1]) + (block[2] + block[3])
        for k in range(8):
            gradient = total[k * 10 : (k + 1) * 10, :]
            groups[h, k] = gradient
            kept = held[h, k].astype(F32)
            value, _, _ = step(gradient / 16.0, kept[0:10, :] + kept[10:20, :], kept[20:30, :], kept[30:40, :])
            rows[k * 10 : (k + 1) * 10, :] = value
        out[...] = rows[...].astype(BF16)
    for y in range(4):
        for h in range(2):
            mine[y, h] = groups[h, 2 * y + info[CORE]].astype(BF16)
            theirs[y, h] = groups[h, 2 * y + 1 - info[CORE]].astype(BF16)


def weights(info, parts, held):
    return call(
        weights_kernel,
        "weights",
        [jax.ShapeDtypeStruct((80, 896), BF16)] * 2 + [jax.ShapeDtypeStruct((4, 2, 10, 896), BF16)] * 2,
        [SMEM] + [VMEM] * 9,
        [VMEM] * 4,
        (info, *parts, held),
        [pltpu.VMEM((80, 896), F32), pltpu.VMEM((2, 8, 10, 896), F32)],
    )


def pack_kernel(info, mine, other, *outs):
    for dy, out in enumerate(outs):
        y = lax.rem(info[Y] + dy, 4)
        out[0] = mine[y]
        out[1] = other[y]


def pack(info, mine, other):
    return call(
        pack_kernel,
        "pack",
        [jax.ShapeDtypeStruct((2, 2, 10, 896), BF16)] * 4,
        [SMEM] + [VMEM] * 2,
        [VMEM] * 4,
        (info, mine, other),
    )


def update_kernel(info, *refs):
    parts, (master, first, second) = refs[:4], refs[4:7]
    new_master, new_first, new_second = refs[7:]
    for dy, part in enumerate(parts):
        for dc in range(2):
            for flip in range(2):
                block = columns(info, -dy, flip, lax.rem(info[CORE] + dc, 2))
                value, moved, spread = step(
                    part[dc, flip].astype(F32) / 16.0, master[block], first[block], second[block]
                )
                new_master[block] = value
                new_first[block] = moved
                new_second[block] = spread


def update(info, parts, master, first, second):
    return call(
        update_kernel,
        "update",
        [jax.ShapeDtypeStruct((10, 14336), F32)] * 3,
        [SMEM] + [VMEM] * 7,
        [VMEM] * 3,
        (info, *parts, master, first, second),
    )


def merge_kernel(info, *refs):
    parts, out, rows = refs[:4], refs[4], refs[5]
    low = info[ZHI] == 0
    for n in range(2):
        mine, far = parts[2 * n][...].astype(F32), parts[2 * n + 1][...].astype(F32)
        for k, block in enumerate((jnp.where(low, mine, far), jnp.where(low, far, mine))):
            for y in range(4):
                at = n * 160 + y * 40 + k * 20
                rows[at : at + 20, :] = block[y * 20 : (y + 1) * 20, :]
    out[...] = rows[...].astype(BF16)


def merge(info, parts):
    return call(
        merge_kernel,
        "merge",
        jax.ShapeDtypeStruct((320, 896), BF16),
        [SMEM] + [VMEM] * 4,
        VMEM,
        (info, *parts),
        [pltpu.VMEM((320, 896), F32)],
    )


def place_kernel(spans, info, *refs):
    blocks, out, sem = refs[: len(refs) - 2], refs[-2], refs[-1]
    spans = list(spans)
    count = 0
    for block in blocks:
        if block.shape == out.shape:
            continue
        for first in range(0, block.shape[0], 160):
            at = pl.multiple_of(info[PLACE + spans[count]], 32)
            pltpu.make_async_copy(
                block.at[pl.ds(first, 160), :], out.at[pl.ds(at, 160), :], sem
            ).start()
            count += 1
    whole = out.at[pl.ds(0, 160 * count), :]
    pltpu.make_async_copy(whole, whole, sem).wait()


def place(info, spans, blocks, before=None):
    old = [] if before is None else [before]
    return pl.pallas_call(
        functools.partial(place_kernel, spans),
        out_shape=jax.ShapeDtypeStruct((2560, 896), BF16),
        in_specs=[SMEM] + [VMEM] * len(blocks) + [ANY] * len(old),
        out_specs=ANY,
        scratch_shapes=[pltpu.SemaphoreType.DMA],
        input_output_aliases={1 + len(blocks): 0} if old else {},
        compiler_params=pltpu.CompilerParams(vmem_limit_bytes=16 * MIB),
        cost_estimate=pl.CostEstimate(flops=0, bytes_accessed=1024, transcendentals=0),
        name="place",
    )(info, *blocks, *old)


def tie(*values):
    return lax.optimization_barrier(values)


def on_device(features, cotangent, master, first_moment, second_moment):
    device = lax.axis_index("rep") * 16 + lax.axis_index("tp")
    info = lax.dynamic_index_in_dim(jnp.asarray(facts()), device, 0, keepdims=False)

    own, half_a, half_b = prepare(info, features)
    held = list(state(info, master, first_moment, second_moment))
    a_here, left, right, own, half_b, held[1], held[3], g = tie(
        send(half_a, dz=4),
        send(own, dy=1),
        send(own, dy=-1),
        own,
        half_b,
        send(held[1], dy=1),
        send(held[3], dy=3),
        fetch(info, cotangent, own),
    )
    b_here, a_left, a_right = send(half_b, dz=4), send(a_here, dy=1), send(a_here, dy=-1)
    opposite_a, opposite_b = send(left[:1280], dy=1), send(right[1280:], dy=-1)
    opposite_a, opposite_b, left, right, a_here = tie(opposite_a, opposite_b, left, right, a_here)
    left_c, right_c, a_here_c = send(left, dc=1), send(right, dc=1), send(a_here, dc=1)
    b_here, a_left, a_right, left_c, right_c, a_here_c, opposite_a, opposite_b, own = tie(
        b_here, a_left, a_right, left_c, right_c, a_here_c, opposite_a, opposite_b, own
    )
    a_two, a_one = send(a_left[:640], dy=1), send(a_right[640:], dy=-1)
    b_here_c = send(b_here, dc=1)
    own_c = send(own, dc=1)
    a_two, a_one, a_left, a_right, opposite_a, opposite_b, b_here, b_here_c, own_c = tie(
        a_two, a_one, a_left, a_right, opposite_a, opposite_b, b_here, b_here_c, own_c
    )
    b_left, b_right = send(b_here, dy=1), send(b_here, dy=-1)
    a_two_c, a_one_c = send(a_two, dc=1), send(a_one, dc=1)
    a_left_c, a_right_c = send(a_left, dc=1), send(a_right, dc=1)
    opposite_a_c, opposite_b_c = send(opposite_a, dc=1), send(opposite_b, dc=1)
    a_two_c, a_one_c, a_left_c, a_right_c, opposite_a_c, opposite_b_c = tie(
        a_two_c, a_one_c, a_left_c, a_right_c, opposite_a_c, opposite_b_c
    )

    def around(dx, *more):
        first = 640 * ACROSS.index(dx)
        pieces = [own, own_c, left, left_c, right, right_c]
        if first < 1280:
            pieces += [opposite_a, opposite_a_c, a_here, a_here_c, a_left, a_left_c, a_right, a_right_c]
        else:
            pieces += [opposite_b, opposite_b_c, b_here, b_here_c, b_left, b_left_c, b_right, b_right_c]
        return [(piece, first % piece.shape[0]) for piece in pieces + list(more)]

    def add(first, *others):
        total = first.astype(F32)
        for other in others:
            total = total + other.astype(F32)
        return total.astype(BF16)

    def cut(total, chunk):
        result = {}
        for i, (j, h) in enumerate(CHUNKS[chunk]):
            part = total[i * 80 : (i + 1) * 80]
            result[j, h] = part if (j, h) == (0, 0) else send_z(part, j, h)
        return result

    two_ac, two_bd = term_rows(2, info, around(2, a_two, a_two_c), g)
    two_ac, two_bd = tie(send(two_ac, dx=1), send(two_bd, dx=-1))
    b_three, b_none = send(b_left[:640], dy=1), send(b_right[640:], dy=-1)
    ahead = term_rows(1, info, around(1, a_one, a_one_c), g)
    b_left, b_right, b_three, b_none, *ahead = tie(b_left, b_right, b_three, b_none, *ahead)
    plain_b = send(ahead[1], dx=1)
    b_left_c, b_right_c = send(b_left, dc=1), send(b_right, dc=1)
    b_three_c, b_none_c = send(b_three, dc=1), send(b_none, dc=1)
    carried_a = add(ahead[0], two_ac[:160])
    behind = term_rows(3, info, around(3, b_three, b_three_c), g)
    plain_a = send(behind[0], dx=-1)
    carried_b = add(behind[1], two_bd[:160])
    carried_a, carried_b = send(carried_a, dx=1), send(carried_b, dx=-1)
    plain_d, plain_c, _, _ = tie(ahead[3], behind[2], two_ac, two_bd)
    plain_d, plain_c = send(plain_d, dx=1), send(plain_c, dx=-1)
    here = term_rows(0, info, around(0, b_none, b_none_c), g)
    carried_c, carried_d = add(ahead[2], two_ac[160:]), add(behind[3], two_bd[160:])
    sum_a, sum_b = add(here[0], plain_a, carried_a), add(here[1], plain_b, carried_b)
    carried_c, carried_d, sum_a, sum_b, held[2] = tie(carried_c, carried_d, sum_a, sum_b, held[2])
    held[2] = send(held[2], dy=2)
    carried_c, carried_d = send(carried_c, dx=1), send(carried_d, dx=-1)
    parts = {**cut(sum_a, 0), **cut(sum_b, 1)}
    plain_c, plain_d, carried_c, carried_d, held[2] = tie(plain_c, plain_d, carried_c, carried_d, held[2])
    parts.update(cut(add(here[2], plain_c, carried_c), 2))
    parts.update(cut(add(here[3], plain_d, carried_d), 3))
    held = arrange(info, held, send(state_core(info, held), dc=1))
    same, other, mine, theirs = weights(info, [parts[j, h] for h in range(2) for j in range(4)], held)

    packed = list(pack(info, mine, send(theirs, dc=1)))
    parts = [send_z(value, j, h) for j in PAIRS[0] for h, value in enumerate((same, other))]
    *parts, same, other, packed[1] = tie(*parts, same, other, send(packed[1], dy=1))
    block = merge(info, parts)
    parts = [same, send_z(other, 0, 1), send_z(same, 2, 0), send_z(other, 2, 1)]
    *parts, left, right, packed[2] = tie(*parts, send(block, dx=1), send(block, dx=-1), packed[2])
    blocks = [block, left, right]
    block = merge(info, parts)
    new_weights = place(info, (0, 1, 2, 3, 4, 5, 8, 9), blocks + [block])
    low, high, left, right, packed[2], packed[3], new_weights = tie(
        send(left[:160], dx=1),
        send(right[160:], dx=-1),
        send(block, dx=1),
        send(block, dx=-1),
        send(packed[2], dy=2),
        send(packed[3], dy=3),
        new_weights,
    )
    blocks = [low, high, left, right, send(left[:160], dx=1), send(right[160:], dx=-1)]
    new_master, new_first, new_second = update(info, packed, master, first_moment, second_moment)
    new_weights = place(info, (6, 7, 10, 11, 12, 13, 14, 15), blocks, new_weights)
    return (new_master, new_first, new_second, new_weights)


def solution(mesh):
    in_specs = (
        P(("rep", "tp"), None),
        P("rep", "tp"),
        P(("rep", "tp"), None),
        P(("rep", "tp"), None),
        P(("rep", "tp"), None),
    )
    out_specs = (
        P(("rep", "tp"), None),
        P(("rep", "tp"), None),
        P(("rep", "tp"), None),
        P(None, "tp"),
    )
    return jax.shard_map(
        on_device, mesh=mesh, in_specs=in_specs, out_specs=out_specs, check_vma=False
    )
```

```python
import functools

import jax
import jax.numpy as jnp
import numpy as np
from jax import lax
from jax.experimental import pallas as pl
from jax.experimental.pallas import tpu as pltpu
from jax.sharding import PartitionSpec as P

STEP = 10

beta_one = 0.9
beta_two = 0.95
outer_rate = 0.05
weight_decay = 0.1
epsilon = 1e-08

BOTH = ("rep", "tp")
BF16, F32 = jnp.bfloat16, jnp.float32
MIB = 1024 * 1024
SMEM = pl.BlockSpec(memory_space=pltpu.SMEM)
VMEM = pl.BlockSpec(memory_space=pltpu.VMEM)
ANY = pl.BlockSpec(memory_space=pl.ANY)

ACROSS = (2, 1, 3, 0)
CHUNKS = (((0, 1), (0, 0)), ((2, 0), (2, 1)), ((1, 0), (1, 1)), ((3, 0), (3, 1)))
ALONE = ((0,), (1,), (2,), (3,))
CUTS = {2: ((0, 2), (1, 3)), 1: ALONE, 3: ALONE, 0: ALONE}
PIECES = tuple((dy, dh, dc) for dh in range(2) for dy in (0, 3, 1, 2) for dc in range(2))
PAIRS = ((1, 3), (0, 2))


def facts():
    rows = []
    for rep in range(16):
        for tp in range(16):
            x, zlo = rep // 4, rep % 4
            row = [x, zlo, tp // 4, tp // 2 % 2, tp % 2]
            row += [
                ((x + dx) % 4 * 4 + (zlo - j) % 4) * 160 for pair in PAIRS for dx in (0, 3, 1, 2) for j in pair
            ]
            y, zhi, core = row[2:5]
            row += [((y + dy) % 4 * 4 + (zhi ^ dh) * 2 + (core ^ dc)) * 128 for dy, dh, dc in PIECES]
            rows.append(row)
    return np.asarray(rows, np.int32)


X, ZLO, Y, ZHI, CORE, PLACE, TOKEN = 0, 1, 2, 3, 4, 5, 21


def pairs(move):
    def index(x, z, y, c):
        x, z, y, c = x % 4, z % 8, y % 4, c % 2
        return (x * 4 + z % 4) * 16 + y * 4 + (z // 4) * 2 + c

    return [
        (index(x, z, y, c), index(*move(x, z, y, c)))
        for x in range(4)
        for z in range(8)
        for y in range(4)
        for c in range(2)
    ]


def send(value, dx=0, dz=0, dy=0, dc=0):
    return lax.ppermute(value, BOTH, pairs(lambda x, z, y, c: (x + dx, z + dz, y + dy, c + dc)))


def send_z(value, j, h):
    def move(x, z, y, c):
        return x, (z // 4 ^ h) * 4 + (z + j) % 4, y, c

    return lax.ppermute(value, BOTH, pairs(move))


def call(kernel, name, out_shape, in_specs, out_specs, args, scratch=(), limit=16, size=1024):
    return pl.pallas_call(
        kernel,
        out_shape=out_shape,
        in_specs=in_specs,
        out_specs=out_specs,
        scratch_shapes=list(scratch),
        compiler_params=pltpu.CompilerParams(vmem_limit_bytes=limit * MIB),
        cost_estimate=pl.CostEstimate(flops=0, bytes_accessed=size, transcendentals=0),
        name=name,
    )(*args)


def prepare_kernel(info, rows, out, half_a, half_b, turned, ordered):
    for k in range(20):
        turned[k * 128 : (k + 1) * 128, :] = rows[:, k * 128 : (k + 1) * 128].astype(F32).T
    at = 0
    for dx in ACROSS:
        for j in range(4):
            start = lax.rem(info[X] + dx, 4) * 640 + lax.rem(info[ZLO] + j, 4) * 160
            for zhi in range(2):
                for y in range(4):
                    ordered[at : at + 20, :] = turned[pl.ds(start + y * 40 + zhi * 20, 20), :]
                    at += 20
    half_a[...] = ordered[:1280, :].astype(BF16)
    half_b[...] = ordered[1280:, :].astype(BF16)
    out[...] = ordered[...].astype(BF16)


def prepare(info, features):
    return call(
        prepare_kernel,
        "prepare",
        [jax.ShapeDtypeStruct((2560, 128), BF16)] + [jax.ShapeDtypeStruct((1280, 128), BF16)] * 2,
        [SMEM, VMEM],
        [VMEM] * 3,
        (info, features),
        [pltpu.VMEM((2560, 128), F32), pltpu.VMEM((2560, 128), F32)],
    )


def fetch_kernel(info, g, _, out):
    for k in range(16):
        start = pl.multiple_of(info[TOKEN + k], 128)
        out[k * 128 : (k + 1) * 128, :] = g[pl.ds(start, 128), :]


def fetch(info, g, after):
    return call(
        fetch_kernel,
        "fetch",
        jax.ShapeDtypeStruct((2048, 896), BF16),
        [SMEM, VMEM, ANY],
        VMEM,
        (info, g, after),
        size=4 * MIB,
    )


def term_kernel(firsts, cuts, info, *refs):
    pieces, g, outs = refs[:16], refs[16], refs[17:]
    low = info[ZHI] == 0
    rows = jnp.concatenate([piece[first : first + 640, :] for piece, first in zip(pieces, firsts)], axis=1)
    for start in range(0, 896, 256):
        stop = min(start + 256, 896)
        total = jnp.dot(rows, g[:, start:stop], preferred_element_type=F32).astype(BF16)
        for out, cut in zip(outs, cuts):
            for k, (j, h) in enumerate(piece for chunk in cut for piece in CHUNKS[chunk]):
                here, there = total[j * 160 : j * 160 + 80, :], total[j * 160 + 80 : j * 160 + 160, :]
                out[k * 80 : (k + 1) * 80, start:stop] = (
                    jnp.where(low, there, here) if h else jnp.where(low, here, there)
                )


def term_rows(dx, info, pieces, g):
    arrays, firsts = zip(*pieces)
    return call(
        functools.partial(term_kernel, firsts, CUTS[dx]),
        "term_rows",
        [jax.ShapeDtypeStruct((160 * len(cut), 896), BF16) for cut in CUTS[dx]],
        [SMEM] + [VMEM] * 17,
        [VMEM] * len(CUTS[dx]),
        (info, *arrays, g),
        limit=24,
    )


def step(pseudo, old, first, second):
    moved = beta_one * first + (1.0 - beta_one) * pseudo
    spread = beta_two * second + (1.0 - beta_two) * pseudo * pseudo
    lead = (beta_one * moved + (1.0 - beta_one) * pseudo) / (1.0 - beta_one ** (STEP + 1))
    scale = spread / (1.0 - beta_two**STEP)
    value = old - outer_rate * (lead / (jnp.sqrt(scale) + epsilon) + weight_decay * old)
    return value, moved, spread


def columns(info, dy, flip, core):
    at = (lax.rem(info[Y] + 4 + dy, 4) * 4 + lax.rem(info[ZHI] + flip, 2) * 2 + core) * 896
    return (slice(None), pl.ds(pl.multiple_of(at, 128), 896))


def state_kernel(info, master, first, second, *refs):
    outs, rows = refs[:4], refs[4]
    for dy, out in enumerate(outs):
        for core in range(2):
            for flip in range(2):
                block = columns(info, dy, flip, core)
                old = master[block]
                top = old.astype(BF16).astype(F32)
                rows[0:10, :] = top
                rows[10:20, :] = old - top
                rows[20:30, :] = first[block]
                rows[30:40, :] = second[block]
                out[core, flip] = rows[...].astype(BF16)


def state(info, master, first, second):
    return call(
        state_kernel,
        "state",
        [jax.ShapeDtypeStruct((2, 2, 40, 896), BF16)] * 4,
        [SMEM] + [VMEM] * 3,
        [VMEM] * 4,
        (info, master, first, second),
        [pltpu.VMEM((40, 896), F32)],
    )


def state_core_kernel(info, *refs):
    parts, out = refs[:4], refs[4]
    for dy, part in enumerate(parts):
        out[lax.rem(info[Y] + 4 - dy, 4)] = part[1 - info[CORE]]


def state_core(info, parts):
    return call(
        state_core_kernel,
        "state_core",
        jax.ShapeDtypeStruct((4, 2, 40, 896), BF16),
        [SMEM] + [VMEM] * 4,
        VMEM,
        (info, *parts),
    )


def arrange_kernel(info, *refs):
    parts, other, out = refs[:4], refs[4], refs[5]
    core = info[CORE]
    for dy, part in enumerate(parts):
        at = lax.rem(info[Y] + 4 - dy, 4) * 2
        for flip in range(2):
            out[flip, at + core] = part[core, flip]
    for y in range(4):
        for flip in range(2):
            out[flip, 2 * y + 1 - core] = other[y, flip]


def arrange(info, parts, other):
    return call(
        arrange_kernel,
        "arrange",
        jax.ShapeDtypeStruct((2, 8, 40, 896), BF16),
        [SMEM] + [VMEM] * 5,
        VMEM,
        (info, *parts, other),
    )


def weights_kernel(info, *refs):
    parts, held, outs, mine, theirs, rows, groups = refs[:8], refs[8], refs[9:11], refs[11], refs[12], refs[13], refs[14]
    for h, out in enumerate(outs):
        block = [parts[4 * h + j][...].astype(F32) for j in range(4)]
        total = (block[0] + block[1]) + (block[2] + block[3])
        for k in range(8):
            gradient = total[k * 10 : (k + 1) * 10, :]
            groups[h, k] = gradient
            kept = held[h, k].astype(F32)
            value, _, _ = step(gradient / 16.0, kept[0:10, :] + kept[10:20, :], kept[20:30, :], kept[30:40, :])
            rows[k * 10 : (k + 1) * 10, :] = value
        out[...] = rows[...].astype(BF16)
    for y in range(4):
        for h in range(2):
            mine[y, h] = groups[h, 2 * y + info[CORE]].astype(BF16)
            theirs[y, h] = groups[h, 2 * y + 1 - info[CORE]].astype(BF16)


def weights(info, parts, held):
    return call(
        weights_kernel,
        "weights",
        [jax.ShapeDtypeStruct((80, 896), BF16)] * 2 + [jax.ShapeDtypeStruct((4, 2, 10, 896), BF16)] * 2,
        [SMEM] + [VMEM] * 9,
        [VMEM] * 4,
        (info, *parts, held),
        [pltpu.VMEM((80, 896), F32), pltpu.VMEM((2, 8, 10, 896), F32)],
    )


def pack_kernel(info, mine, other, *outs):
    for dy, out in enumerate(outs):
        y = lax.rem(info[Y] + dy, 4)
        out[0] = mine[y]
        out[1] = other[y]


def pack(info, mine, other):
    return call(
        pack_kernel,
        "pack",
        [jax.ShapeDtypeStruct((2, 2, 10, 896), BF16)] * 4,
        [SMEM] + [VMEM] * 2,
        [VMEM] * 4,
        (info, mine, other),
    )


def update_kernel(info, *refs):
    parts, (master, first, second) = refs[:4], refs[4:7]
    new_master, new_first, new_second = refs[7:]
    for dy, part in enumerate(parts):
        for dc in range(2):
            for flip in range(2):
                block = columns(info, -dy, flip, lax.rem(info[CORE] + dc, 2))
                value, moved, spread = step(
                    part[dc, flip].astype(F32) / 16.0, master[block], first[block], second[block]
                )
                new_master[block] = value
                new_first[block] = moved
                new_second[block] = spread


def update(info, parts, master, first, second):
    return call(
        update_kernel,
        "update",
        [jax.ShapeDtypeStruct((10, 14336), F32)] * 3,
        [SMEM] + [VMEM] * 7,
        [VMEM] * 3,
        (info, *parts, master, first, second),
    )


def merge_kernel(info, *refs):
    parts, out, rows = refs[:4], refs[4], refs[5]
    low = info[ZHI] == 0
    for n in range(2):
        mine, far = parts[2 * n][...].astype(F32), parts[2 * n + 1][...].astype(F32)
        for k, block in enumerate((jnp.where(low, mine, far), jnp.where(low, far, mine))):
            for y in range(4):
                at = n * 160 + y * 40 + k * 20
                rows[at : at + 20, :] = block[y * 20 : (y + 1) * 20, :]
    out[...] = rows[...].astype(BF16)


def merge(info, parts):
    return call(
        merge_kernel,
        "merge",
        jax.ShapeDtypeStruct((320, 896), BF16),
        [SMEM] + [VMEM] * 4,
        VMEM,
        (info, *parts),
        [pltpu.VMEM((320, 896), F32)],
    )


def place_kernel(spans, info, *refs):
    blocks, out, sem = refs[: len(refs) - 2], refs[-2], refs[-1]
    spans = list(spans)
    count = 0
    for block in blocks:
        if block.shape == out.shape:
            continue
        for first in range(0, block.shape[0], 160):
            at = pl.multiple_of(info[PLACE + spans[count]], 32)
            pltpu.make_async_copy(
                block.at[pl.ds(first, 160), :], out.at[pl.ds(at, 160), :], sem
            ).start()
            count += 1
    whole = out.at[pl.ds(0, 160 * count), :]
    pltpu.make_async_copy(whole, whole, sem).wait()


def place(info, spans, blocks, before=None):
    old = [] if before is None else [before]
    return pl.pallas_call(
        functools.partial(place_kernel, spans),
        out_shape=jax.ShapeDtypeStruct((2560, 896), BF16),
        in_specs=[SMEM] + [VMEM] * len(blocks) + [ANY] * len(old),
        out_specs=ANY,
        scratch_shapes=[pltpu.SemaphoreType.DMA],
        input_output_aliases={1 + len(blocks): 0} if old else {},
        compiler_params=pltpu.CompilerParams(vmem_limit_bytes=16 * MIB),
        cost_estimate=pl.CostEstimate(flops=0, bytes_accessed=1024, transcendentals=0),
        name="place",
    )(info, *blocks, *old)


def tie(*values):
    return lax.optimization_barrier(values)


def on_device(features, cotangent, master, first_moment, second_moment):
    device = lax.axis_index("rep") * 16 + lax.axis_index("tp")
    info = lax.dynamic_index_in_dim(jnp.asarray(facts()), device, 0, keepdims=False)

    own, half_a, half_b = prepare(info, features)
    held = list(state(info, master, first_moment, second_moment))
    a_here, left, right, own, half_b, held[1], held[3], g = tie(
        send(half_a, dz=4),
        send(own, dy=1),
        send(own, dy=-1),
        own,
        half_b,
        send(held[1], dy=1),
        send(held[3], dy=3),
        fetch(info, cotangent, own),
    )
    b_here, a_left, a_right = send(half_b, dz=4), send(a_here, dy=1), send(a_here, dy=-1)
    opposite_a, opposite_b = send(left[:1280], dy=1), send(right[1280:], dy=-1)
    opposite_a, opposite_b, left, right, a_here = tie(opposite_a, opposite_b, left, right, a_here)
    left_c, right_c, a_here_c = send(left, dc=1), send(right, dc=1), send(a_here, dc=1)
    b_here, a_left, a_right, left_c, right_c, a_here_c, opposite_a, opposite_b, own = tie(
        b_here, a_left, a_right, left_c, right_c, a_here_c, opposite_a, opposite_b, own
    )
    a_two, a_one = send(a_left[:640], dy=1), send(a_right[640:], dy=-1)
    b_here_c = send(b_here, dc=1)
    own_c = send(own, dc=1)
    a_two, a_one, a_left, a_right, opposite_a, opposite_b, b_here, b_here_c, own_c = tie(
        a_two, a_one, a_left, a_right, opposite_a, opposite_b, b_here, b_here_c, own_c
    )
    b_left, b_right = send(b_here, dy=1), send(b_here, dy=-1)
    a_two_c, a_one_c = send(a_two, dc=1), send(a_one, dc=1)
    a_left_c, a_right_c = send(a_left, dc=1), send(a_right, dc=1)
    opposite_a_c, opposite_b_c = send(opposite_a, dc=1), send(opposite_b, dc=1)
    a_two_c, a_one_c, a_left_c, a_right_c, opposite_a_c, opposite_b_c = tie(
        a_two_c, a_one_c, a_left_c, a_right_c, opposite_a_c, opposite_b_c
    )

    def around(dx, *more):
        first = 640 * ACROSS.index(dx)
        pieces = [own, own_c, left, left_c, right, right_c]
        if first < 1280:
            pieces += [opposite_a, opposite_a_c, a_here, a_here_c, a_left, a_left_c, a_right, a_right_c]
        else:
            pieces += [opposite_b, opposite_b_c, b_here, b_here_c, b_left, b_left_c, b_right, b_right_c]
        return [(piece, first % piece.shape[0]) for piece in pieces + list(more)]

    def add(first, *others):
        total = first.astype(F32)
        for other in others:
            total = total + other.astype(F32)
        return total.astype(BF16)

    def cut(total, chunk):
        result = {}
        for i, (j, h) in enumerate(CHUNKS[chunk]):
            part = total[i * 80 : (i + 1) * 80]
            result[j, h] = part if (j, h) == (0, 0) else send_z(part, j, h)
        return result

    two_ac, two_bd = term_rows(2, info, around(2, a_two, a_two_c), g)
    two_ac, two_bd = tie(send(two_ac, dx=1), send(two_bd, dx=-1))
    b_three, b_none = send(b_left[:640], dy=1), send(b_right[640:], dy=-1)
    ahead = term_rows(1, info, around(1, a_one, a_one_c), g)
    b_left, b_right, b_three, b_none, *ahead = tie(b_left, b_right, b_three, b_none, *ahead)
    plain_b = send(ahead[1], dx=1)
    b_left_c, b_right_c = send(b_left, dc=1), send(b_right, dc=1)
    b_three_c, b_none_c = send(b_three, dc=1), send(b_none, dc=1)
    carried_a = add(ahead[0], two_ac[:160])
    behind = term_rows(3, info, around(3, b_three, b_three_c), g)
    plain_a = send(behind[0], dx=-1)
    carried_b = add(behind[1], two_bd[:160])
    carried_a, carried_b = send(carried_a, dx=1), send(carried_b, dx=-1)
    plain_d, plain_c, _, _ = tie(ahead[3], behind[2], two_ac, two_bd)
    plain_d, plain_c = send(plain_d, dx=1), send(plain_c, dx=-1)
    here = term_rows(0, info, around(0, b_none, b_none_c), g)
    carried_c, carried_d = add(ahead[2], two_ac[160:]), add(behind[3], two_bd[160:])
    sum_a, sum_b = add(here[0], plain_a, carried_a), add(here[1], plain_b, carried_b)
    carried_c, carried_d, sum_a, sum_b, held[2] = tie(carried_c, carried_d, sum_a, sum_b, held[2])
    held[2] = send(held[2], dy=2)
    carried_c, carried_d = send(carried_c, dx=1), send(carried_d, dx=-1)
    parts = {**cut(sum_a, 0), **cut(sum_b, 1)}
    plain_c, plain_d, carried_c, carried_d, held[2] = tie(plain_c, plain_d, carried_c, carried_d, held[2])
    parts.update(cut(add(here[2], plain_c, carried_c), 2))
    parts.update(cut(add(here[3], plain_d, carried_d), 3))
    held = arrange(info, held, send(state_core(info, held), dc=1))
    same, other, mine, theirs = weights(info, [parts[j, h] for h in range(2) for j in range(4)], held)

    packed = list(pack(info, mine, send(theirs, dc=1)))
    parts = [send_z(value, j, h) for j in PAIRS[0] for h, value in enumerate((same, other))]
    *parts, same, other, packed[1] = tie(*parts, same, other, send(packed[1], dy=1))
    block = merge(info, parts)
    parts = [same, send_z(other, 0, 1), send_z(same, 2, 0), send_z(other, 2, 1)]
    *parts, left, right, packed[2] = tie(*parts, send(block, dx=1), send(block, dx=-1), packed[2])
    blocks = [block, left, right]
    block = merge(info, parts)
    new_weights = place(info, (0, 1, 2, 3, 4, 5, 8, 9), blocks + [block])
    low, high, left, right, packed[2], packed[3], new_weights = tie(
        send(left[:160], dx=1),
        send(right[160:], dx=-1),
        send(block, dx=1),
        send(block, dx=-1),
        send(packed[2], dy=2),
        send(packed[3], dy=3),
        new_weights,
    )
    blocks = [low, high, left, right, send(left[:160], dx=1), send(right[160:], dx=-1)]
    new_master, new_first, new_second = update(info, packed, master, first_moment, second_moment)
    new_weights = place(info, (6, 7, 10, 11, 12, 13, 14, 15), blocks, new_weights)
    return (new_master, new_first, new_second, new_weights)


def solution(mesh):
    in_specs = (
        P(("rep", "tp"), None),
        P("rep", "tp"),
        P(("rep", "tp"), None),
        P(("rep", "tp"), None),
        P(("rep", "tp"), None),
    )
    out_specs = (
        P(("rep", "tp"), None),
        P(("rep", "tp"), None),
        P(("rep", "tp"), None),
        P(None, "tp"),
    )
    return jax.shard_map(
        on_device, mesh=mesh, in_specs=in_specs, out_specs=out_specs, check_vma=False
    )
```
